512 devices in a mesh: patch: 128 (over z, y_lo, x), prompt: 4 (over y_hi, core).
Axes of the slice: x: 4, y: 8 (y_hi: 2, y_lo: 4; y = y_hi * 4 + y_lo), z: 8, core: 2. Of those that a mesh axis runs over, the one named last changes fastest.
Arguments:
- x_first: bfloat16 [1024, 8, 320], P(('prompt', 'patch')), parts along dimension 0, may hold values from -240 to 240
- x_second: bfloat16 [1024, 8, 320], P(('prompt', 'patch')), parts along dimension 0, may hold values from -240 to 240
- timesteps: int32 [2], replicated, may hold values from 0 to 999
- conv_kernel: bfloat16 [640, 9, 320], P('patch'), may hold values from -0.109375 to 0.109375
- skip_weight: bfloat16 [320, 640], replicated, may hold values from -0.13378906 to 0.13378906
- time_weight: bfloat16 [320, 640], replicated, may hold values from -0.5 to 0.5
- gain_in: float32 [320], replicated, may hold values from 0.25 to 1.75
- shift_in: float32 [320], replicated, may hold values from -1 to 1
- gain_mid: float32 [640], replicated, may hold values from 0.25 to 1.75
- shift_mid: float32 [640], replicated, may hold values from -1 to 1
- query_weight: bfloat16 [640, 320], replicated, may hold values from -0.25 to 0.25
- key_weight: bfloat16 [640, 320], replicated, may hold values from -0.25 to 0.25
- value_weight: bfloat16 [640, 320], replicated, may hold values from -0.25 to 0.25
- out_weight: bfloat16 [320, 640], replicated, may hold values from -0.3125 to 0.3125
Outputs:
- out_first: bfloat16 [1024, 8, 640], P(('prompt', 'patch')), parts along dimension 0
- out_second: bfloat16 [1024, 8, 640], P(('prompt', 'patch')), parts along dimension 0
The draws below stay inside these ranges and needn't reach their ends.
There are 4 independent parts, one for each index of `prompt`. The reference program is written for one: setup_inputs(seed, part) draws one part's arguments, and reference() takes and returns one part's arrays. A program takes and returns all parts, laid end to end along the dimension named above; an argument that names none is the same for every part. Nothing has to cross between parts.
All inputs are finite; a program needn't handle non-finite values.
Results may differ from the reference program's by a relative error of at most 0.025.
Values may be sent and summed in bfloat16 or wider, within the bound.
No kernel may reach another device: no remote copies, remote signals or barrier semaphores. Data moves between devices by JAX's collectives and lax.ppermute only.
A program may use at most 64 MiB of HBM per device.

```python
import math
import jax
import jax.numpy as jnp
from jax import lax

C_IN = 320
C = 640
HEADS = 5
HEAD_DIM = 64
GROUPS = 32
ROWS_DEV = 2
COLS = 8
STEPS = 2
ROWS = 256
N_PATCH = 128


def spike_marks(key):
    return jax.random.randint(key, (8,), 0, ROWS * COLS)


def shaped(key, marks, base, slope, boost):
    normal_key = jax.random.fold_in(key, 0)
    normal_part = jnp.clip(jax.random.normal(normal_key, (ROWS, COLS, C_IN), jnp.float32), -4.0, 4.0)
    noise = normal_part
    position = jnp.arange(ROWS, dtype=jnp.float32) / max(ROWS - 1, 1)
    scale = base + slope * position
    token = jnp.arange(ROWS * COLS)
    hit = jnp.any(token[:, None] == marks[None, :], axis=1).reshape(ROWS, COLS)
    factor = jnp.where(hit, boost, 1.0)
    values = noise * scale[:, None, None] * factor[:, :, None] + position[:, None, None]
    return jnp.clip(values, -240.0, 240.0)


def draw_x_first(key, part):
    marks = spike_marks(key)
    key = jax.random.fold_in(key, 3)
    return shaped(key, marks, 0.5, 3.0, 1.0).astype(jnp.bfloat16)


def draw_x_second(key, part):
    marks = spike_marks(key)
    key = jax.random.fold_in(key, 7)
    return shaped(key, marks, 0.5, 3.0, 1.0).astype(jnp.bfloat16)


def block_levels(own_key, shape, cuts, low, high):
    level = 1.0
    for dim, parts in cuts:
        steps = jax.random.uniform(jax.random.fold_in(jax.random.fold_in(own_key, 6), dim), (parts,), jnp.float32, low / len(cuts), high / len(cuts))
        level = level * jnp.repeat(jnp.exp(steps), shape[dim] // parts).reshape((-1,) + (1,) * (len(shape) - 1 - dim))
    return level


def centred(own_key, shape, scale, most, shards=(), kind=jnp.bfloat16):
    level = block_levels(own_key, shape, shards, -0.22, 0.18) if shards else 1.0
    drawn = jax.random.normal(own_key, shape, jnp.float32) * scale * level
    return jnp.minimum(jnp.maximum(drawn, -most), most).astype(kind)


def setup_inputs(seed: int = 0, part: int = 0) -> dict:
    splits = jax.random.split(jax.random.key(seed), 15)
    part_splits = jax.random.split(jax.random.fold_in(splits[14], part), 15)
    return {
        "x_first": draw_x_first(jax.random.fold_in(jax.random.fold_in(splits[14], part), 71), part),
        "x_second": draw_x_second(jax.random.fold_in(jax.random.fold_in(splits[14], part), 71), part),
        "timesteps": jax.random.randint(splits[2], (STEPS,), 0, 1000).astype(jnp.int32),
        "conv_kernel": centred(splits[3], (C, 9, C_IN), (9 * C_IN) ** -0.5, 0.109375, ((0, 128),)),
        "skip_weight": centred(splits[4], (C_IN, C), (0.4 * C_IN ** -0.5), 0.13378906),
        "time_weight": centred(splits[5], (C_IN, C), (C_IN // 2) ** -0.5, 0.5),
        "gain_in": jnp.clip(1.0 + 0.15 * jax.random.normal(splits[6], (C_IN,), jnp.float32), 0.25, 1.75),
        "shift_in": jnp.clip(jax.random.uniform(splits[7], (C_IN,), jnp.float32, -1.0, 1.0), -1.0, 1.0),
        "gain_mid": jnp.clip(1.0 + 0.15 * jax.random.normal(splits[8], (C,), jnp.float32), 0.25, 1.75),
        "shift_mid": jnp.clip(jax.random.uniform(splits[9], (C,), jnp.float32, -1.0, 1.0), -1.0, 1.0),
        "query_weight": centred(splits[10], (C, HEADS * HEAD_DIM), C ** -0.5, 0.25),
        "key_weight": centred(splits[11], (C, HEADS * HEAD_DIM), C ** -0.5, 0.25),
        "value_weight": centred(splits[12], (C, HEADS * HEAD_DIM), C ** -0.5, 0.25),
        "out_weight": centred(splits[13], (HEADS * HEAD_DIM, C), (HEADS * HEAD_DIM) ** -0.5, 0.3125),
    }


norm_eps = 1e-05

def group_sums(flat, groups):
    values = flat.astype(jnp.float32).reshape(flat.shape[0], groups, -1)
    return (lax.optimization_barrier(jnp.sum(values, axis=(0, 2))), lax.optimization_barrier(jnp.sum(values * values, axis=(0, 2))))

def normalize(flat, sums, squares, count, gain, shift):
    groups = sums.shape[0]
    mean = sums / count
    spread = squares / count - mean * mean
    values = flat.astype(jnp.float32).reshape(flat.shape[0], groups, -1)
    values = (values - mean[None, :, None]) * lax.rsqrt(spread + norm_eps)[None, :, None]
    return values.reshape(flat.shape[0], -1) * gain + shift

def conv_taps(upper, middle, lower):
    width = middle.shape[1]
    taps = []
    for source in (upper, middle, lower):
        padded = jnp.pad(source, ((0, 0), (1, 1), (0, 0)))
        for shift_col in range(3):
            taps.append(padded[:, shift_col:shift_col + width])
    stacked = jnp.stack(taps, axis=2)
    return stacked.reshape(middle.shape[0] * width, -1)

def time_features(steps_int, width):
    half = width // 2
    freqs = jnp.exp(-math.log(10000.0) * jnp.arange(half, dtype=jnp.float32) / half)
    angles = steps_int.astype(jnp.float32)[:, None] * freqs[None, :]
    return jnp.concatenate([jnp.cos(angles), jnp.sin(angles)], axis=1)

def attend(query, keys, values, heads):
    count = query.shape[0]
    head_size = query.shape[1] // heads
    qf = query.astype(jnp.float32).reshape(count, heads, head_size)
    kf = keys.astype(jnp.float32).reshape(keys.shape[0], heads, head_size)
    vf = values.astype(jnp.float32).reshape(values.shape[0], heads, head_size)
    scores = jnp.einsum('qhd,khd->hqk', qf, kf) / math.sqrt(head_size)
    top = lax.optimization_barrier(jnp.max(scores, axis=-1, keepdims=True))
    weights = jnp.exp(scores - top)
    denom = lax.optimization_barrier(jnp.sum(weights, axis=-1))
    rounded = lax.optimization_barrier(weights.astype(jnp.bfloat16)).astype(jnp.float32)
    mixed = jnp.einsum('hqk,khd->qhd', rounded, vf)
    mixed = mixed / jnp.transpose(denom)[:, :, None]
    return mixed.reshape(count, -1).astype(jnp.bfloat16)

def reference(x_first, x_second, timesteps, conv_kernel, skip_weight, time_weight, gain_in, shift_in, gain_mid, shift_mid, query_weight, key_weight, value_weight, out_weight):
    tok_dev = ROWS_DEV * COLS
    keys_all = ROWS * COLS
    flat1 = x_first.reshape(keys_all, C_IN)
    flat2 = x_second.reshape(keys_all, C_IN)
    count_in = keys_all * (C_IN // GROUPS)
    s1, q1 = group_sums(flat1, GROUPS)
    s2, q2 = group_sums(flat2, GROUPS)
    act1 = jax.nn.silu(normalize(flat1, s1, q1, count_in, gain_in, shift_in)).astype(jnp.bfloat16).reshape(ROWS, COLS, C_IN)
    act2 = jax.nn.silu(normalize(flat2, s2, q2, count_in, gain_in, shift_in)).astype(jnp.bfloat16).reshape(ROWS, COLS, C_IN)
    zero_row = jnp.zeros((1, COLS, C_IN), jnp.bfloat16)
    up1 = jnp.concatenate([zero_row, act1[:-1]], axis=0)
    down1 = jnp.concatenate([act1[1:], zero_row], axis=0)
    row_ids = jnp.arange(ROWS)
    top_edge = (row_ids % ROWS_DEV == 0)[:, None, None]
    bottom_edge = (row_ids % ROWS_DEV == ROWS_DEV - 1)[:, None, None]
    up2 = jnp.where(top_edge, up1, jnp.concatenate([zero_row, act2[:-1]], axis=0))
    down2 = jnp.where(bottom_edge, down1, jnp.concatenate([act2[1:], zero_row], axis=0))
    kernel_flat = conv_kernel.reshape(C, 9 * C_IN)
    dims = (((1,), (1,)), ((), ()))
    conv1 = lax.dot_general(conv_taps(up1, act1, down1), kernel_flat, dims, preferred_element_type=jnp.float32)
    conv2 = lax.dot_general(conv_taps(up2, act2, down2), kernel_flat, dims, preferred_element_type=jnp.float32)
    feats = jax.nn.silu(time_features(timesteps, C_IN))
    shifts = jnp.dot(feats, time_weight.astype(jnp.float32), precision=lax.Precision.HIGHEST)
    h1 = (jnp.dot(flat1, skip_weight, preferred_element_type=jnp.float32) + conv1 + shifts[0][None, :]).astype(jnp.bfloat16)
    h2 = (jnp.dot(flat2, skip_weight, preferred_element_type=jnp.float32) + conv2 + shifts[1][None, :]).astype(jnp.bfloat16)
    count_mid = keys_all * (C // GROUPS)
    hs1, hq1 = group_sums(h1, GROUPS)
    hs2, hq2 = group_sums(h2, GROUPS)
    m1 = normalize(h1, hs1, hq1, count_mid, gain_mid, shift_mid).astype(jnp.bfloat16)
    m2 = normalize(h2, hs2, hq2, count_mid, gain_mid, shift_mid).astype(jnp.bfloat16)

    def project(m, weight):
        return jnp.dot(m, weight, preferred_element_type=jnp.float32).astype(jnp.bfloat16)
    qa1, ka1, va1 = (project(m1, query_weight), project(m1, key_weight), project(m1, value_weight))
    qa2, ka2, va2 = (project(m2, query_weight), project(m2, key_weight), project(m2, value_weight))
    owner = jnp.arange(keys_all) // tok_dev

    def per_patch(index):
        start = (index * tok_dev).astype(jnp.int32)
        qb1 = lax.dynamic_slice_in_dim(qa1, start, tok_dev, 0)
        qb2 = lax.dynamic_slice_in_dim(qa2, start, tok_dev, 0)
        own = (owner == index)[:, None]
        keys2 = jnp.where(own, ka2, ka1)
        vals2 = jnp.where(own, va2, va1)
        return (attend(qb1, ka1, va1, HEADS), attend(qb2, keys2, vals2, HEADS))
    o1, o2 = lax.map(per_patch, jnp.arange(N_PATCH, dtype=jnp.int32))
    o1 = o1.reshape(keys_all, -1)
    o2 = o2.reshape(keys_all, -1)
    out1 = (h1.astype(jnp.float32) + jnp.dot(o1, out_weight, preferred_element_type=jnp.float32)).astype(jnp.bfloat16)
    out2 = (h2.astype(jnp.float32) + jnp.dot(o2, out_weight, preferred_element_type=jnp.float32)).astype(jnp.bfloat16)
    return (out1.reshape(ROWS, COLS, C), out2.reshape(ROWS, COLS, C))
```

```python
import functools
import math

import jax
import jax.numpy as jnp
from jax import lax
from jax.experimental import pallas as pl
from jax.experimental.pallas import tpu as pltpu
from jax.sharding import Mesh, PartitionSpec as P

F32 = jnp.float32
BF16 = jnp.bfloat16
HEADS = 5
HEAD = 64
GROUPS = 32
C_IN = 320
C = 640
ATT = HEADS * HEAD
EPS = 1e-05
NZY = 32
NX = 4
TOK = 16
CX = C // NX
KEYS = NZY * NX * TOK
KEYS_PAD = KEYS + 128
COUNT_IN = float(KEYS * (C_IN // GROUPS))
COUNT_MID = float(KEYS * (C // GROUPS))
BLK = 48
LAST = NZY * TOK + 32
HIGH = lax.Precision.HIGHEST
NT = (((1,), (1,)), ((), ()))
VMEM_LIMIT = 48 * 1024 * 1024


def iota(shape, dim):
    return lax.broadcasted_iota(jnp.int32, shape, dim)


def pieces(row):
    hi = row.astype(BF16).astype(F32)
    mid = (row - hi).astype(BF16).astype(F32)
    lo = (row - hi - mid).astype(BF16).astype(F32)
    return hi, mid, lo


def fold_sums(rows, select):
    wide = jnp.dot(rows, select, precision=HIGH, preferred_element_type=F32)
    keep = (iota((8, 128), 1) >> 5) == iota((8, 128), 0)
    return jnp.sum(jnp.where(keep, wide, 0.0), axis=0, keepdims=True)


def spread_sums(line, select):
    keep = (iota((8, 128), 1) >> 5) == iota((8, 128), 0)
    rows = jnp.where(keep, jnp.broadcast_to(line, (8, 128)), 0.0)
    return jnp.dot(rows, select, precision=HIGH, preferred_element_type=F32)


def in_select(shape, group_dim, channel_dim):
    group = iota(shape, group_dim) & 31
    channel = iota(shape, channel_dim)
    return ((channel >= 10 * group) & (channel < 10 * group + 10)).astype(F32)


def mid_select(shape):
    return ((iota(shape, 0) & 31) == (iota(shape, 1) & 31)).astype(F32)


def slab_select(shape, x, dtype):
    row = iota(shape, 0)
    target = 20 * (row & 31) + 5 * x + (row >> 5)
    return (target == iota(shape, 1)).astype(dtype)


def pack_kernel_body(x1_ref, x2_ref, ker_ref, out_ref, rows_ref):
    for k in range(5):
        rows_ref[9 * k : 9 * k + 9, :] = ker_ref[k].astype(F32)
    x1 = x1_ref[...].astype(F32)
    x2 = x2_ref[...].astype(F32)
    sums = [jnp.sum(v, axis=0, keepdims=True) for v in (x1, x1 * x1, x2, x2 * x2)]
    sums = jnp.concatenate(sums + [jnp.zeros((4, C_IN), F32)], axis=0)
    line = fold_sums(sums, in_select((C_IN, 128), 1, 0))
    rows_ref[45:48, :] = jnp.zeros((3, C_IN), F32)
    hi, mid, lo = pieces(line)
    rows_ref[45:46, 0:128] = hi
    rows_ref[46:47, 0:128] = mid
    rows_ref[47:48, 0:128] = lo
    block = rows_ref[...].astype(BF16)

    def put(i, carry):
        out_ref[i] = block
        return carry

    lax.fori_loop(0, NZY, put, 0)


def tokens_body(part_ref, x1_ref, x2_ref, halo_ref, out_ref):
    part = jnp.sum(part_ref[...].astype(F32), axis=0)
    line = jnp.sum(part[13:16, :], axis=0, keepdims=True)
    hi, mid, lo = pieces(line)
    stats = jnp.concatenate([hi, mid, lo, jnp.zeros((5, 128), F32)], axis=0)
    stats = jnp.concatenate([stats, jnp.zeros((8, C_IN - 128), F32)], axis=1)
    tail = jnp.concatenate([halo_ref[...].astype(F32), stats], axis=0).astype(BF16)
    for i in range(NX):
        out_ref[i, 0:16, :] = x1_ref[...]
        out_ref[i, 16:32, :] = x2_ref[...]
        out_ref[i, 32:48, :] = tail


def prep_body(idx_ref, feats_ref, tw_ref, sw_ref, qw_ref, kw_ref, vw_ref, gm_ref, sm_ref, w_ref, sk_ref, tm_ref, gs_ref):
    x = idx_ref[1]
    mine = slab_select((CX, C), x, F32)
    time = jnp.dot(feats_ref[...], tw_ref[...].astype(F32), precision=HIGH, preferred_element_type=F32)
    tm_ref[...] = lax.dot_general(time, mine, NT, precision=HIGH, preferred_element_type=F32)
    sk_ref[...] = lax.dot_general(sw_ref[...], mine.astype(BF16), NT, preferred_element_type=F32).astype(BF16)
    w_ref[...] = jnp.zeros(w_ref.shape, BF16)
    both = jnp.concatenate([gm_ref[...], sm_ref[...], jnp.zeros((6, C), F32)], axis=0)
    for i in range(NX):
        slab = slab_select((CX, C), i, BF16)
        for n, ref in enumerate((qw_ref, kw_ref, vw_ref)):
            part = jnp.dot(slab, ref[...], preferred_element_type=F32)
            w_ref[i, :, 384 * n : 384 * n + ATT] = part.astype(BF16)
        lane = iota((C, C), 0)
        lane = lane - CX * ((lane >= CX).astype(jnp.int32) + (lane >= 2 * CX).astype(jnp.int32) + (lane >= 3 * CX).astype(jnp.int32))
        target = 20 * (lane & 31) + 5 * i + (lane >> 5)
        wide = (target == iota((C, C), 1)).astype(F32)
        gs_ref[i] = lax.dot_general(both, wide, NT, precision=HIGH, preferred_element_type=F32)


def conv_body(idx_ref, ker_ref, tok_ref, skip_ref, time_ref, gain_ref, shift_ref, send_ref, h2_ref, ker_f32, lanes_ref):
    zy = idx_ref[0]
    for part in range(3):
        width = 128 if part < 2 else 64

        def widen(i, carry):
            at = pl.multiple_of(i * BLK, BLK)
            ker_f32[part, pl.ds(at, BLK), 0:width] = ker_ref[i, :, 128 * part : 128 * part + width].astype(F32)
            return carry

        lax.fori_loop(0, NZY, widen, 0)
    stats = jnp.zeros((1, 128), F32)
    for j in range(NX):
        stats = stats + jnp.sum(tok_ref[j, 32:48, 0:128].astype(F32)[8:11], axis=0, keepdims=True)
    wide = spread_sums(stats, in_select((128, C_IN), 0, 1)) / COUNT_IN
    gain = gain_ref[...]
    shift = shift_ref[...]

    def act(values, s):
        mean = wide[2 * s : 2 * s + 1]
        spread = wide[2 * s + 1 : 2 * s + 2] - mean * mean
        n = (values - mean) * lax.rsqrt(spread + EPS) * gain + shift
        n = n / (1.0 + jnp.exp(-n))
        return n.astype(BF16).astype(F32)

    x1 = jnp.concatenate([tok_ref[j, 0:16, :] for j in range(NX)], axis=0)
    x2 = jnp.concatenate([tok_ref[j, 16:32, :] for j in range(NX)], axis=0)
    top = tok_ref[0, 32:48, :].astype(F32)[0:8]
    bottom = tok_ref[NX - 1, 32:48, :].astype(F32)[0:8]
    a1 = act(x1.astype(F32), 0)
    a2 = act(x2.astype(F32), 1)
    top = jnp.where(zy == 0, 0.0, act(top, 0))
    bottom = jnp.where(zy == NZY - 1, 0.0, act(bottom, 0))
    a1 = jnp.concatenate([top, a1, bottom], axis=0)

    def columns(a):
        n = a.shape[0]
        col = iota(a.shape, 0) & 7
        left = jnp.where(col == 0, 0.0, pltpu.roll(a, 1, 0))
        right = jnp.where(col == 7, 0.0, pltpu.roll(a, n - 1, 0))
        return (left, a, right)

    cols1 = columns(a1)
    cols2 = columns(a2)
    rows = 2 * NX
    acc = jnp.dot(jnp.concatenate([x1, x2], axis=0), skip_ref[...], preferred_element_type=F32)
    conv = jnp.zeros((2 * NX * TOK, CX), F32)
    for dy in range(3):
        for dx in range(3):
            b1, b2 = cols1[dx], cols2[dx]
            first = b1[8 * dy : 8 * dy + 8 * rows]
            tiles = []
            for r in range(rows):
                stale = (dy == 0 and r % 2 == 0) or (dy == 2 and r % 2 == 1)
                at = r + dy - 1
                tiles.append(b1[8 * at + 8 : 8 * at + 16] if stale else b2[8 * at : 8 * at + 8])
            taps = jnp.concatenate([first] + tiles, axis=0).astype(BF16)
            t = 3 * dy + dx
            slab = []
            for k in range(5):
                strips = [ker_f32[part, pl.ds(9 * k + t, NZY, stride=BLK), :] for part in range(3)]
                slab.append(jnp.concatenate(strips, axis=1)[:, :C_IN])
            slab = jnp.concatenate(slab, axis=0).astype(BF16)
            conv = conv + lax.dot_general(taps, slab, NT, preferred_element_type=F32)
    half = NX * TOK
    step = iota((2 * half, 1), 0) >= half
    h = acc + conv + jnp.where(step, time_ref[1:2, :], time_ref[0:1, :])
    h = h.astype(BF16).astype(F32)
    h2 = h[half:]
    sums = jnp.concatenate(
        [jnp.sum(h2, axis=0, keepdims=True), jnp.sum(h2 * h2, axis=0, keepdims=True), jnp.zeros((6, CX), F32)], axis=0
    )
    hi, mid, lo = pieces(fold_sums(sums, mid_select((CX, 128))))
    lanes_ref[:, C:] = jnp.concatenate([hi, mid, lo, jnp.zeros((13, 128), F32)], axis=0)
    lanes_ref[:, :C] = jnp.concatenate([h[TOK * j : TOK * j + TOK] for j in range(NX)], axis=1)
    block = lanes_ref[...].astype(BF16)
    h2_ref[...] = jnp.concatenate([h2[TOK * j : TOK * j + TOK] for j in range(NX)], axis=1).astype(BF16)

    def put(i, carry):
        send_ref[i] = block
        return carry

    lax.fori_loop(0, NZY, put, 0)


def relay_body(part_ref, h2_ref, out_ref):
    line = jnp.zeros((1, 128), F32)
    total = jnp.sum(part_ref[:, :, C:].astype(F32), axis=0)
    line = jnp.sum(total[0:3], axis=0, keepdims=True)
    hi, mid, lo = pieces(line)
    stats = jnp.concatenate([hi, mid, lo, jnp.zeros((13, 128), F32)], axis=0)
    stats = jnp.concatenate([stats, jnp.zeros((TOK, C - 128), F32)], axis=1).astype(BF16)
    for i in range(NX):
        out_ref[i, NZY * TOK : NZY * TOK + TOK, :] = h2_ref[...]
        out_ref[i, NZY * TOK + TOK : LAST, :] = stats

    def put(g, carry):
        at = pl.multiple_of(g * TOK, TOK)
        block = part_ref[g, :, 0:C]
        for i in range(NX):
            out_ref[i, pl.ds(at, TOK), :] = block
        return carry

    lax.fori_loop(0, NZY, put, 0)


def attend_body(idx_ref, h_ref, w_ref, gs_ref, ow_ref, o1_ref, o2_ref, kk_ref, vv_ref):
    zy = idx_ref[0]
    x = idx_ref[1]
    chunk = 128
    steps = NZY * TOK // chunk

    def add_up(c, carry):
        total, square = carry
        at = pl.multiple_of(c * chunk, chunk)
        for i in range(NX):
            h = h_ref[i, pl.ds(at, chunk), :].astype(F32)
            total = total + jnp.sum(h.reshape(chunk // 8, 8, C), axis=0)
            square = square + jnp.sum((h * h).reshape(chunk // 8, 8, C), axis=0)
        return total, square

    zero = jnp.zeros((8, C), F32)
    total, square = lax.fori_loop(0, steps, add_up, (zero, zero))
    first = jnp.concatenate(
        [jnp.sum(total, axis=0, keepdims=True), jnp.sum(square, axis=0, keepdims=True), jnp.zeros((6, C), F32)], axis=0
    )
    first = jnp.dot(first, mid_select((C, C)), precision=HIGH, preferred_element_type=F32) / COUNT_MID
    mean1 = first[0:1]
    rstd1 = lax.rsqrt(first[1:2] - mean1 * mean1 + EPS)
    line = jnp.zeros((1, 128), F32)
    for i in range(NX):
        line = line + jnp.sum(h_ref[i, NZY * TOK + TOK : LAST, 0:128].astype(F32)[0:3], axis=0, keepdims=True)
    second = spread_sums(line, mid_select((128, CX))) / COUNT_MID
    mean2 = second[0:1]
    rstd2 = lax.rsqrt(second[1:2] - mean2 * mean2 + EPS)

    def project(c, carry):
        at = pl.multiple_of(c * chunk, chunk)
        ms = []
        for i in range(NX):
            h = h_ref[i, pl.ds(at, chunk), :].astype(F32)
            ms.append((((h - mean1) * rstd1) * gs_ref[i, 0:1, :] + gs_ref[i, 1:2, :]).astype(BF16))
        for j in range(NX):
            kv = jnp.zeros((chunk, 768), F32)
            for i in range(NX):
                kv = kv + jnp.dot(ms[i][:, CX * j : CX * j + CX], w_ref[i, :, 384:1152], preferred_element_type=F32)
            to = pl.multiple_of(j * NZY * TOK + at, chunk)
            kk_ref[pl.ds(to, chunk), :] = kv[:, 0:ATT].astype(BF16)
            vv_ref[pl.ds(to, chunk), :] = kv[:, 384 : 384 + ATT].astype(BF16)
        return carry

    lax.fori_loop(0, steps, project, 0)
    own = pl.multiple_of(zy * TOK, TOK)
    qkv = jnp.zeros((2 * TOK, 1152), F32)
    base = jnp.zeros((2 * TOK, C), F32)
    second_row = iota((2 * TOK, 1), 0) >= TOK
    for i in range(NX):
        both = jnp.concatenate([h_ref[i, pl.ds(own, TOK), :], h_ref[i, NZY * TOK : NZY * TOK + TOK, :]], axis=0).astype(F32)
        mine = both[:, 0:CX]
        for j in range(1, NX):
            mine = jnp.where(x == j, both[:, CX * j : CX * j + CX], mine)
        mean = jnp.where(second_row, mean2, mean1[:, 0:CX])
        rstd = jnp.where(second_row, rstd2, rstd1[:, 0:CX])
        m = ((mine - mean) * rstd * gs_ref[i, 0:1, 0:CX] + gs_ref[i, 1:2, 0:CX]).astype(BF16)
        qkv = qkv + jnp.dot(m, w_ref[i], preferred_element_type=F32)
        base = base + jnp.dot(mine.astype(BF16), slab_select((CX, C), i, BF16), preferred_element_type=F32)
    qkv = qkv.astype(BF16)
    kk_ref[KEYS : KEYS + TOK, :] = qkv[TOK:, 384 : 384 + ATT]
    vv_ref[KEYS : KEYS + TOK, :] = qkv[TOK:, 768 : 768 + ATT]
    kk_ref[KEYS + TOK :, :] = jnp.zeros((KEYS_PAD - KEYS - TOK, ATT), BF16)
    vv_ref[KEYS + TOK :, :] = jnp.zeros((KEYS_PAD - KEYS - TOK, ATT), BF16)
    rows = HEADS * 2 * TOK
    q = qkv[:, 0:ATT].astype(F32) * (1.0 / math.sqrt(HEAD))
    q = jnp.concatenate([q] * HEADS, axis=0)
    head = (iota((rows, ATT), 1) >> 6) == (iota((rows, ATT), 0) >> 5)
    q = jnp.where(head, q, 0.0).astype(BF16)
    scores = lax.dot_general(q, kk_ref[...], NT, preferred_element_type=F32)
    col = iota((rows, KEYS_PAD), 1)
    later = ((iota((rows, KEYS_PAD), 0) >> 4) & 1) == 1
    low = x * (NZY * TOK) + zy * TOK
    own_col = (col >= low) & (col < low + TOK)
    valid = (col < KEYS) & jnp.logical_not(later & own_col)
    valid = valid | (later & (col >= KEYS) & (col < KEYS + TOK))
    scores = jnp.where(valid, scores, -1e30)
    top = jnp.max(scores, axis=1, keepdims=True)
    weights = jnp.exp(scores - top)
    denom = jnp.sum(weights, axis=1, keepdims=True)
    mixed = jnp.dot(weights.astype(BF16), vv_ref[...], preferred_element_type=F32)
    mixed = jnp.where(head, mixed / denom, 0.0)
    out = mixed[0 : 2 * TOK]
    for n in range(1, HEADS):
        out = out + mixed[2 * TOK * n : 2 * TOK * n + 2 * TOK]
    result = base + jnp.dot(out.astype(BF16), ow_ref[...], preferred_element_type=F32)
    result = result.astype(BF16)
    o1_ref[...] = result[0:TOK]
    o2_ref[...] = result[TOK:]


def call(body, out_shape, in_specs, scratch=(), cost=None):
    many = isinstance(out_shape, (list, tuple))
    vmem = pl.BlockSpec(memory_space=pltpu.VMEM)
    return pl.pallas_call(
        body,
        out_shape=out_shape,
        in_specs=in_specs,
        out_specs=[vmem] * len(out_shape) if many else vmem,
        scratch_shapes=list(scratch),
        compiler_params=pltpu.CompilerParams(vmem_limit_bytes=VMEM_LIMIT),
        cost_estimate=cost,
    )


def shape(dims, dtype=BF16):
    return jax.ShapeDtypeStruct(dims, dtype)


def spread(blocks, axis):
    return lax.all_to_all(blocks, axis, 0, 0, tiled=True)


def time_features(steps_int, width):
    half = width // 2
    freqs = jnp.exp(-math.log(10000.0) * jnp.arange(half, dtype=F32) / half)
    angles = steps_int.astype(F32)[:, None] * freqs[None, :]
    return jnp.concatenate([jnp.cos(angles), jnp.sin(angles)], axis=1)


def per_device(
    x_first,
    x_second,
    timesteps,
    conv_kernel,
    skip_weight,
    time_weight,
    gain_in,
    shift_in,
    gain_mid,
    shift_mid,
    query_weight,
    key_weight,
    value_weight,
    out_weight,
):
    vmem = pl.BlockSpec(memory_space=pltpu.VMEM)
    smem = pl.BlockSpec(memory_space=pltpu.SMEM)
    zy = lax.axis_index("zy")
    x = lax.axis_index("x")
    idx = jnp.stack([zy, x]).astype(jnp.int32)
    x1 = x_first.reshape(TOK, C_IN)
    x2 = x_second.reshape(TOK, C_IN)

    first = call(pack_kernel_body, shape((NZY, BLK, C_IN)), [vmem] * 3, [pltpu.VMEM((BLK, C_IN), F32)])(x1, x2, conv_kernel)
    edge = jnp.where(x == NX - 1, x_first[1], x_first[0])
    pairs = []
    for g in range(NZY - 1):
        pairs += [(NX * g + NX - 1, NX * g + NX), (NX * g + NX, NX * g + NX - 1)]
    halo = lax.ppermute(edge, ("zy", "x"), pairs)
    kernels = spread(first, "zy")

    feats = jax.nn.silu(time_features(timesteps, C_IN))
    feats = jnp.pad(feats, ((0, 6), (0, 0)))
    weights, skip_slab, time_slab, scale_mid = call(
        prep_body,
        [shape((NX, CX, 1152)), shape((C_IN, CX)), shape((8, CX), F32), shape((NX, 8, C), F32)],
        [smem] + [vmem] * 8,
        cost=pl.CostEstimate(flops=2 * 640 * 640 * 1200, bytes_accessed=4 << 20, transcendentals=0),
    )(idx, feats, time_weight, skip_weight, query_weight, key_weight, value_weight, gain_mid[None], shift_mid[None])

    tokens = pl.pallas_call(
        tokens_body,
        grid=(1,),
        out_shape=shape((NX, BLK, C_IN)),
        in_specs=[
            pl.BlockSpec((NZY, 16, 128), lambda i: (0, 2, 0)),
            pl.BlockSpec((TOK, C_IN), lambda i: (0, 0)),
            pl.BlockSpec((TOK, C_IN), lambda i: (0, 0)),
            pl.BlockSpec((8, C_IN), lambda i: (0, 0)),
        ],
        out_specs=pl.BlockSpec((NX, BLK, C_IN), lambda i: (0, 0, 0)),
        compiler_params=pltpu.CompilerParams(vmem_limit_bytes=VMEM_LIMIT),
    )(kernels, x1, x2, halo)
    tokens = spread(tokens, "x")

    send, h2 = call(
        conv_body,
        [shape((NZY, TOK, C + 128)), shape((TOK, C))],
        [smem] + [vmem] * 6,
        [pltpu.VMEM((3, NZY * BLK, 128), F32), pltpu.VMEM((TOK, C + 128), F32)],
    )(idx, kernels, tokens, skip_slab, time_slab, gain_in[None], shift_in[None])
    gathered = spread(send, "zy")
    relayed = call(relay_body, shape((NX, LAST, C)), [vmem] * 2)(gathered, h2)
    everything = spread(relayed, "x")
    out1, out2 = call(
        attend_body,
        [shape((TOK, C)), shape((TOK, C))],
        [smem] + [vmem] * 4,
        [pltpu.VMEM((KEYS_PAD, ATT), BF16), pltpu.VMEM((KEYS_PAD, ATT), BF16)],
    )(idx, everything, weights, scale_mid, out_weight)
    rows = x_first.shape[:2]
    return out1.reshape(*rows, C), out2.reshape(*rows, C)


def solution(mesh):
    prompts = mesh.shape["prompt"]
    grid = Mesh(mesh.devices.reshape(NZY, NX, prompts), ("zy", "x", "prompt"))
    tokens = P(("prompt", "zy", "x"), None, None)
    return jax.shard_map(
        per_device,
        mesh=grid,
        in_specs=(tokens, tokens, P(), P(("zy", "x"), None, None)) + (P(),) * 10,
        out_specs=(tokens, tokens),
        check_vma=False,
    )
```

```python
import functools
import math

import jax
import jax.numpy as jnp
from jax import lax
from jax.experimental import pallas as pl
from jax.experimental.pallas import tpu as pltpu
from jax.sharding import Mesh, PartitionSpec as P

F32 = jnp.float32
BF16 = jnp.bfloat16
HEADS = 5
HEAD = 64
GROUPS = 32
C_IN = 320
C = 640
ATT = HEADS * HEAD
EPS = 1e-05
NB = 16
NA = 8
TOK = 16
CX = C // NA
KEYS = NB * NA * TOK
COUNT_IN = float(KEYS * (C_IN // GROUPS))
COUNT_MID = float(KEYS * (C // GROUPS))
BLK = 48
HALF = C_IN // 2
KEYS_DEV = NB * TOK
KEYS_PAD = KEYS_DEV + 128
PACK = KEYS_DEV // NA
RELAY = PACK + 3 * TOK
HIGH = lax.Precision.HIGHEST
NT = (((1,), (1,)), ((), ()))
VMEM_LIMIT = 48 * 1024 * 1024


def iota(shape, dim):
    return lax.broadcasted_iota(jnp.int32, shape, dim)


def pieces(row):
    hi = row.astype(BF16).astype(F32)
    mid = (row - hi).astype(BF16).astype(F32)
    lo = (row - hi - mid).astype(BF16).astype(F32)
    return hi, mid, lo


def fold_sums(rows, select):
    wide = jnp.dot(rows, select, precision=HIGH, preferred_element_type=F32)
    keep = (iota((8, 128), 1) >> 5) == iota((8, 128), 0)
    return jnp.sum(jnp.where(keep, wide, 0.0), axis=0, keepdims=True)


def spread_sums(line, select):
    keep = (iota((8, 128), 1) >> 5) == iota((8, 128), 0)
    rows = jnp.where(keep, jnp.broadcast_to(line, (8, 128)), 0.0)
    return jnp.dot(rows, select, precision=HIGH, preferred_element_type=F32)


def in_select(shape, group_dim, channel_dim):
    group = iota(shape, group_dim) & 31
    channel = iota(shape, channel_dim)
    return ((channel >= 10 * group) & (channel < 10 * group + 10)).astype(F32)


def mid_select(shape, group_dim, a):
    group = iota(shape, group_dim) & 31
    lane = iota(shape, 1 - group_dim)
    return (group == 2 * (lane & 15) + (a >> 2)).astype(F32)


def slab_select(shape, x, dtype):
    row = iota(shape, 0)
    target = 40 * (row & 15) + 5 * x + (row >> 4)
    return (target == iota(shape, 1)).astype(dtype)


def pack_kernel_body(idx_ref, x1_ref, x2_ref, ker_ref, out_ref, rows_ref, lanes_ref):
    core = idx_ref[2]
    for k in range(5):
        both = ker_ref[k].astype(F32)
        rows_ref[9 * k : 9 * k + 9, :] = jnp.where(core == 0, both[:, :HALF], both[:, HALF:])
    x1 = x1_ref[...].astype(F32)
    x2 = x2_ref[...].astype(F32)
    sums = [jnp.sum(v, axis=0, keepdims=True) for v in (x1, x1 * x1, x2, x2 * x2)]
    sums = jnp.concatenate(sums + [jnp.zeros((4, C_IN), F32)], axis=0)
    line = fold_sums(sums, in_select((C_IN, 128), 1, 0))
    thirds = [rows_ref[15 * b : 15 * b + 15, :] for b in range(3)]
    lanes_ref[0:15, :] = jnp.concatenate(thirds + [jnp.zeros((15, 32), F32)], axis=1)
    lanes_ref[15:16, :] = jnp.concatenate(list(pieces(line)) + [jnp.zeros((1, 128), F32)], axis=1)
    block = lanes_ref[...].astype(BF16)

    def put(i, carry):
        out_ref[i] = block
        return carry

    lax.fori_loop(0, NB, put, 0)


def tokens_body(part_ref, x1_ref, x2_ref, halo_ref, after_ref, out_ref, again_ref):
    again_ref[...] = part_ref[...]
    part = jnp.sum(part_ref[:, :, 0:384].astype(F32), axis=0)[15:16]
    hi, mid, lo = pieces(part[:, 0:128] + part[:, 128:256] + part[:, 256:384])
    stats = jnp.concatenate([hi, mid, lo, jnp.zeros((5, 128), F32)], axis=0)
    stats = jnp.concatenate([stats, jnp.zeros((8, C_IN - 128), F32)], axis=1)
    tail = jnp.concatenate([halo_ref[...].astype(F32), stats], axis=0).astype(BF16)
    for i in range(NA):
        out_ref[i, 0:16, :] = x1_ref[...]
        out_ref[i, 16:32, :] = x2_ref[...]
        out_ref[i, 32:48, :] = tail


def prep_body(idx_ref, feats_ref, tw_ref, sw_ref, qw_ref, kw_ref, vw_ref, gm_ref, sm_ref, w_ref, sk_ref, tm_ref, gs_ref):
    x = idx_ref[1]
    mine = slab_select((CX, C), x, F32)
    time = jnp.dot(feats_ref[...], tw_ref[...].astype(F32), precision=HIGH, preferred_element_type=F32)
    tm_ref[...] = lax.dot_general(time, mine, NT, precision=HIGH, preferred_element_type=F32)
    sk_ref[...] = lax.dot_general(sw_ref[...], mine.astype(BF16), NT, preferred_element_type=F32).astype(BF16)
    w_ref[...] = jnp.zeros(w_ref.shape, BF16)
    both = jnp.concatenate([gm_ref[...], sm_ref[...], jnp.zeros((6, C), F32)], axis=0)
    for i in range(NA):
        slab = slab_select((CX, C), i, BF16)
        for n, ref in enumerate((qw_ref, kw_ref, vw_ref)):
            part = jnp.dot(slab, ref[...], preferred_element_type=F32)
            w_ref[i, :, 384 * n : 384 * n + ATT] = part.astype(BF16)
        wide = slab_select((CX, C), i, F32)
        part = lax.dot_general(both, wide, NT, precision=HIGH, preferred_element_type=F32)
        gs_ref[i] = jnp.concatenate([part] * NA, axis=1)


def conv_body(idx_ref, ker_ref, far_ref, tok_ref, skip_ref, time_ref, gain_ref, shift_ref, send_ref, h2_ref, ker_f32, lanes_ref):
    b = idx_ref[0]
    core = idx_ref[2]
    for n, ref in enumerate((ker_ref, far_ref)):
        for strip in range(4):
            ker_f32[n, strip] = ref[:, :, 128 * strip : 128 * strip + 128].astype(F32).reshape(NB * TOK, 128)
    stats = jnp.zeros((1, 128), F32)
    for j in range(NA):
        stats = stats + jnp.sum(tok_ref[j, 32:48, 0:128].astype(F32)[8:11], axis=0, keepdims=True)
    wide = spread_sums(stats, in_select((128, C_IN), 0, 1)) / COUNT_IN
    gain = gain_ref[...]
    shift = shift_ref[...]

    def act(values, s):
        mean = wide[2 * s : 2 * s + 1]
        spread = wide[2 * s + 1 : 2 * s + 2] - mean * mean
        n = (values - mean) * lax.rsqrt(spread + EPS) * gain + shift
        n = n / (1.0 + jnp.exp(-n))
        return n.astype(BF16).astype(F32)

    x1 = jnp.concatenate([tok_ref[j, 0:16, :] for j in range(NA)], axis=0)
    x2 = jnp.concatenate([tok_ref[j, 16:32, :] for j in range(NA)], axis=0)
    top = tok_ref[0, 32:48, :].astype(F32)[0:8]
    bottom = tok_ref[NA - 1, 32:48, :].astype(F32)[0:8]
    a1 = act(x1.astype(F32), 0)
    a2 = act(x2.astype(F32), 1)
    top = jnp.where(b == 0, 0.0, act(top, 0))
    bottom = jnp.where(b == NB - 1, 0.0, act(bottom, 0))
    a1 = jnp.concatenate([top, a1, bottom], axis=0)

    def near_first(a):
        swapped = jnp.concatenate([a[:, HALF:], a[:, :HALF]], axis=1)
        return jnp.where(core == 0, a, swapped)

    a1 = near_first(a1)
    a2 = near_first(a2)

    def columns(a):
        n = a.shape[0]
        col = iota(a.shape, 0) & 7
        left = jnp.where(col == 0, 0.0, pltpu.roll(a, 1, 0))
        right = jnp.where(col == 7, 0.0, pltpu.roll(a, n - 1, 0))
        return (left, a, right)

    cols1 = columns(a1)
    cols2 = columns(a2)
    rows = 2 * NA
    acc = jnp.dot(jnp.concatenate([x1, x2], axis=0), skip_ref[...], preferred_element_type=F32)
    conv = jnp.zeros((2 * NA * TOK, CX), F32)
    for dy in range(3):
        for dx in range(3):
            b1, b2 = cols1[dx], cols2[dx]
            first = b1[8 * dy : 8 * dy + 8 * rows]
            tiles = []
            for r in range(rows):
                stale = (dy == 0 and r % 2 == 0) or (dy == 2 and r % 2 == 1)
                at = r + dy - 1
                tiles.append(b1[8 * at + 8 : 8 * at + 16] if stale else b2[8 * at : 8 * at + 8])
            taps = jnp.concatenate([first] + tiles, axis=0).astype(BF16)
            t = 3 * dy + dx
            slab = []
            for k in range(5):
                third, row = divmod(9 * k + t, 15)
                strip, off = divmod(HALF * third, 128)
                ends = []
                for n in range(2):
                    pair = [ker_f32[n, strip + e, pl.ds(row, NB, stride=TOK), :] for e in range(2)]
                    ends.append(jnp.concatenate(pair, axis=1)[:, off : off + HALF])
                slab.append(jnp.concatenate(ends, axis=1))
            slab = jnp.concatenate(slab, axis=0).astype(BF16)
            conv = conv + lax.dot_general(taps, slab, NT, preferred_element_type=F32)
    half = NA * TOK
    step = iota((2 * half, 1), 0) >= half
    h = acc + conv + jnp.where(step, time_ref[1:2, :], time_ref[0:1, :])
    h = h.astype(BF16).astype(F32)
    h2 = h[half:]
    sums = [jnp.sum(h2, axis=0, keepdims=True), jnp.sum(h2 * h2, axis=0, keepdims=True)]
    sums = jnp.concatenate([jnp.zeros((2, CX), F32)] + sums + [jnp.zeros((4, CX), F32)], axis=0)
    hi, mid, lo = pieces(fold_sums(sums, mid_select((CX, 128), 1, idx_ref[1])))
    lanes_ref[:, C:] = jnp.concatenate([hi, mid, lo, jnp.zeros((13, 128), F32)], axis=0)
    lanes_ref[:, :C] = jnp.concatenate([h[TOK * j : TOK * j + TOK] for j in range(NA)], axis=1)
    block = lanes_ref[...].astype(BF16)
    h2_ref[...] = jnp.concatenate([h2[TOK * j : TOK * j + TOK] for j in range(NA)], axis=1).astype(BF16)

    def put(i, carry):
        send_ref[i] = block
        return carry

    lax.fori_loop(0, NB, put, 0)


def relay_body(idx_ref, part_ref, h2_ref, out_ref):
    b = idx_ref[0]

    def put(i, carry):
        total, square = carry
        at = pl.multiple_of(i * TOK, TOK)
        blocks = []
        for n in range(NA):
            block = part_ref[(NB // NA) * n + i, :, 0:C].astype(F32)
            total = total + block
            square = square + block * block
            blocks.append(block)
        for d in range(NA):
            packed = jnp.concatenate([block[:, CX * d : CX * d + CX] for block in blocks], axis=1)
            out_ref[d, pl.ds(at, TOK), :] = packed.astype(BF16)
        return total, square

    zero = jnp.zeros((TOK, C), F32)
    total, square = lax.fori_loop(0, NB // NA, put, (zero, zero))
    sums = [jnp.sum(total, axis=0, keepdims=True), jnp.sum(square, axis=0, keepdims=True), jnp.zeros((6, C), F32)]
    line = fold_sums(jnp.concatenate(sums, axis=0), mid_select((C, 128), 1, idx_ref[1]))
    arrived = jnp.sum(part_ref[:, :, C:].astype(F32), axis=0)
    line = line + jnp.sum(arrived[0:3], axis=0, keepdims=True)
    hi, mid, lo = pieces(line)
    stats = jnp.concatenate([hi, mid, lo, jnp.zeros((13, 128), F32)], axis=0)
    stats = jnp.concatenate([stats, jnp.zeros((TOK, C - 128), F32)], axis=1).astype(BF16)
    mine = part_ref[b, :, 0:C]
    for d in range(NA):
        out_ref[d, PACK : PACK + TOK, :] = mine
        out_ref[d, PACK + TOK : PACK + 2 * TOK, :] = h2_ref[...]
        out_ref[d, PACK + 2 * TOK : RELAY, :] = stats


def attend_body(idx_ref, h_ref, w_ref, gs_ref, send_ref, base_ref, kk_ref, vv_ref):
    b = idx_ref[0]
    x = idx_ref[1]
    line = jnp.zeros((1, 128), F32)
    for i in range(NA):
        line = line + jnp.sum(h_ref[i, PACK + 2 * TOK : RELAY, 0:128].astype(F32)[0:3], axis=0, keepdims=True)
    stats = []
    for parity in range(2):
        wide = spread_sums(line, mid_select((128, C), 0, 4 * parity)) / COUNT_MID
        mean1, mean2 = wide[0:1], wide[2:3]
        rstd1 = lax.rsqrt(wide[1:2] - mean1 * mean1 + EPS)
        rstd2 = lax.rsqrt(wide[3:4] - mean2 * mean2 + EPS)
        stats.append(((mean1, rstd1), (mean2, rstd2)))

    def norm(h, step, i):
        mean, rstd = stats[i // 4][step]
        return (((h - mean) * rstd) * gs_ref[i, 0:1, :] + gs_ref[i, 1:2, :]).astype(BF16).astype(F32)

    def part(h, j):
        return h[:, CX * j : CX * j + CX]

    def pick(h):
        mine = part(h, 0)
        for j in range(1, NA):
            mine = jnp.where(x == j, part(h, j), mine)
        return mine

    def stack(blocks):
        return jnp.concatenate(blocks, axis=0).astype(BF16)

    keys = jnp.zeros((KEYS_DEV, 768), F32)
    queries = jnp.zeros((NA * 2 * TOK, 384), F32)
    fresh = jnp.zeros((TOK, 768), F32)
    base = jnp.zeros((2 * TOK, C), F32)
    for i in range(NA):
        m = norm(h_ref[i, 0:PACK, :].astype(F32), 0, i)
        m = stack([part(m, n) for n in range(NA)])
        keys = keys + jnp.dot(m, w_ref[i, :, 384:1152], preferred_element_type=F32)
        h1 = h_ref[i, PACK : PACK + TOK, :].astype(F32)
        h2 = h_ref[i, PACK + TOK : PACK + 2 * TOK, :].astype(F32)
        m1 = norm(h1, 0, i)
        m2 = norm(h2, 1, i)
        rows = []
        for j in range(NA):
            rows += [part(m1, j), part(m2, j)]
        queries = queries + jnp.dot(stack(rows), w_ref[i, :, 0:384], preferred_element_type=F32)
        fresh = fresh + jnp.dot(pick(m2).astype(BF16), w_ref[i, :, 384:1152], preferred_element_type=F32)
        own = stack([pick(h1), pick(h2)])
        base = base + jnp.dot(own, slab_select((CX, C), i, BF16), preferred_element_type=F32)
    base_ref[...] = base
    kk_ref[0:KEYS_DEV, :] = keys[:, 0:ATT].astype(BF16)
    vv_ref[0:KEYS_DEV, :] = keys[:, 384 : 384 + ATT].astype(BF16)
    kk_ref[KEYS_DEV : KEYS_DEV + TOK, :] = fresh[:, 0:ATT].astype(BF16)
    vv_ref[KEYS_DEV : KEYS_DEV + TOK, :] = fresh[:, 384 : 384 + ATT].astype(BF16)
    kk_ref[KEYS_DEV + TOK :, :] = jnp.zeros((KEYS_PAD - KEYS_DEV - TOK, ATT), BF16)
    vv_ref[KEYS_DEV + TOK :, :] = jnp.zeros((KEYS_PAD - KEYS_DEV - TOK, ATT), BF16)
    each = NA * 2 * TOK
    rows = HEADS * each
    q = queries[:, 0:ATT].astype(BF16).astype(F32) * (1.0 / math.sqrt(HEAD))
    lane_head = iota((each, ATT), 1) >> 6
    q = jnp.concatenate([jnp.where(lane_head == n, q, 0.0) for n in range(HEADS)], axis=0).astype(BF16)
    scores = lax.dot_general(q, kk_ref[...], NT, preferred_element_type=F32)
    col = iota((rows, KEYS_PAD), 1)
    row = iota((rows, KEYS_PAD), 0)
    later = (((row >> 4) & 1) == 1) & (((row >> 5) & (NA - 1)) == x)
    low = b * TOK
    stale = later & (col >= low) & (col < low + TOK)
    new = later & (col >= KEYS_DEV) & (col < KEYS_DEV + TOK)
    valid = ((col < KEYS_DEV) & jnp.logical_not(stale)) | new
    scores = jnp.where(valid, scores, -1e30)
    top = jnp.max(scores, axis=1, keepdims=True)
    weights = jnp.exp(scores - top)
    denom = jnp.sum(weights, axis=1, keepdims=True)
    mixed = jnp.dot(weights.astype(BF16), vv_ref[...], preferred_element_type=F32)
    out = jnp.zeros((each, ATT), F32)
    side = jnp.zeros((each, HEAD), F32)
    place = iota((each, HEAD), 1)
    for n in range(HEADS):
        at = slice(each * n, each * n + each)
        out = jnp.where(lane_head == n, mixed[at], out)
        side = jnp.where(place == n, top[at], side)
        side = jnp.where(place == 8 + n, denom[at], side)
    out = jnp.concatenate([out, side], axis=1)
    for j in range(NA):
        send_ref[j] = out[2 * TOK * j : 2 * TOK * j + 2 * TOK]


def combine_body(part_ref, base_ref, ow_ref, o1_ref, o2_ref):
    sides = [part_ref[i, :, ATT:] for i in range(NA)]
    top = sides[0]
    for i in range(1, NA):
        top = jnp.maximum(top, sides[i])
    lane_head = iota((2 * TOK, ATT), 1) >> 6

    def widen(values, at):
        out = jnp.zeros((2 * TOK, ATT), F32)
        for n in range(HEADS):
            out = jnp.where(lane_head == n, values[:, at + n : at + n + 1], out)
        return out

    top = widen(top, 0)
    mixed = jnp.zeros((2 * TOK, ATT), F32)
    denom = jnp.zeros((2 * TOK, ATT), F32)
    for i in range(NA):
        factor = jnp.exp(widen(sides[i], 0) - top)
        mixed = mixed + part_ref[i, :, 0:ATT] * factor
        denom = denom + widen(sides[i], 8) * factor
    out = (mixed / denom).astype(BF16)
    result = base_ref[...] + jnp.dot(out, ow_ref[...], preferred_element_type=F32)
    result = result.astype(BF16)
    o1_ref[...] = result[0:TOK]
    o2_ref[...] = result[TOK:]


def call(body, out_shape, in_specs, scratch=(), cost=None):
    many = isinstance(out_shape, (list, tuple))
    vmem = pl.BlockSpec(memory_space=pltpu.VMEM)
    return pl.pallas_call(
        body,
        out_shape=out_shape,
        in_specs=in_specs,
        out_specs=[vmem] * len(out_shape) if many else vmem,
        scratch_shapes=list(scratch),
        compiler_params=pltpu.CompilerParams(vmem_limit_bytes=VMEM_LIMIT),
        cost_estimate=cost,
    )


def shape(dims, dtype=BF16):
    return jax.ShapeDtypeStruct(dims, dtype)


def spread(blocks, axis):
    return lax.all_to_all(blocks, axis, 0, 0, tiled=True)


def time_features(steps_int, width):
    half = width // 2
    freqs = jnp.exp(-math.log(10000.0) * jnp.arange(half, dtype=F32) / half)
    angles = steps_int.astype(F32)[:, None] * freqs[None, :]
    return jnp.concatenate([jnp.cos(angles), jnp.sin(angles)], axis=1)


def per_device(
    x_first,
    x_second,
    timesteps,
    conv_kernel,
    skip_weight,
    time_weight,
    gain_in,
    shift_in,
    gain_mid,
    shift_mid,
    query_weight,
    key_weight,
    value_weight,
    out_weight,
):
    vmem = pl.BlockSpec(memory_space=pltpu.VMEM)
    smem = pl.BlockSpec(memory_space=pltpu.SMEM)
    b = lax.axis_index("b")
    x = lax.axis_index("a")
    idx = jnp.stack([b, x, lax.axis_index("core")]).astype(jnp.int32)
    x1 = x_first.reshape(TOK, C_IN)
    x2 = x_second.reshape(TOK, C_IN)

    first = call(
        pack_kernel_body,
        shape((NB, TOK, 512)),
        [smem] + [vmem] * 3,
        [pltpu.VMEM((BLK, HALF), F32), pltpu.VMEM((TOK, 512), F32)],
    )(idx, x1, x2, conv_kernel)
    edge = jnp.where(x == NA - 1, x_first[1], x_first[0])
    pairs = []
    for g in range(NB - 1):
        pairs += [(NA * g + NA - 1, NA * g + NA), (NA * g + NA, NA * g + NA - 1)]
    halo = lax.ppermute(edge, ("b", "a"), pairs)
    kernels = spread(first, "b")

    feats = jax.nn.silu(time_features(timesteps, C_IN))
    feats = jnp.pad(feats, ((0, 6), (0, 0)))
    weights, skip_slab, time_slab, scale_mid = call(
        prep_body,
        [shape((NA, CX, 1152)), shape((C_IN, CX)), shape((8, CX), F32), shape((NA, 8, C), F32)],
        [smem] + [vmem] * 8,
        cost=pl.CostEstimate(flops=2 * 640 * 640 * 1200, bytes_accessed=4 << 20, transcendentals=0),
    )(idx, feats, time_weight, skip_weight, query_weight, key_weight, value_weight, gain_mid[None], shift_mid[None])

    tokens, again = call(tokens_body, [shape((NA, BLK, C_IN)), shape((NB, TOK, 512))], [vmem] * 5)(
        kernels, x1, x2, halo, time_slab
    )
    far = lax.ppermute(again, "core", [(0, 1), (1, 0)])
    tokens = spread(tokens, "a")

    send, h2 = call(
        conv_body,
        [shape((NB, TOK, C + 128)), shape((TOK, C))],
        [smem] + [vmem] * 7,
        [pltpu.VMEM((2, 4, NB * TOK, 128), F32), pltpu.VMEM((TOK, C + 128), F32)],
    )(idx, kernels, far, tokens, skip_slab, time_slab, gain_in[None], shift_in[None])
    gathered = spread(send, "b")
    relayed = call(relay_body, shape((NA, RELAY, C)), [smem] + [vmem] * 2)(idx, gathered, h2)
    everything = spread(relayed, "a")
    partial, base = call(
        attend_body,
        [shape((NA, 2 * TOK, ATT + HEAD), F32), shape((2 * TOK, C), F32)],
        [smem] + [vmem] * 3,
        [pltpu.VMEM((KEYS_PAD, ATT), BF16), pltpu.VMEM((KEYS_PAD, ATT), BF16)],
    )(idx, everything, weights, scale_mid)
    partial = spread(partial, "a")
    out1, out2 = call(combine_body, [shape((TOK, C)), shape((TOK, C))], [vmem] * 3)(partial, base, out_weight)
    rows = x_first.shape[:2]
    return out1.reshape(*rows, C), out2.reshape(*rows, C)


def solution(mesh):
    grid = Mesh(mesh.devices.reshape(NB, NA, 2, 2), ("b", "a", "y_hi", "core"))
    tokens = P(("y_hi", "core", "b", "a"), None, None)
    return jax.shard_map(
        per_device,
        mesh=grid,
        in_specs=(tokens, tokens, P(), P(("b", "a"), None, None)) + (P(),) * 10,
        out_specs=(tokens, tokens),
        check_vma=False,
    )
```

```python
import functools
import math

import jax
import jax.numpy as jnp
from jax import lax
from jax.experimental import pallas as pl
from jax.experimental.pallas import tpu as pltpu
from jax.sharding import Mesh, PartitionSpec as P

F32 = jnp.float32
BF16 = jnp.bfloat16
HEADS = 5
HEAD = 64
GROUPS = 32
C_IN = 320
C = 640
ATT = HEADS * HEAD
EPS = 1e-05
NB = 16
NA = 8
TOK = 16
CX = C // NA
KEYS = NB * NA * TOK
COUNT_IN = float(KEYS * (C_IN // GROUPS))
COUNT_MID = float(KEYS * (C // GROUPS))
BLK = 48
HALF = C_IN // 2
KEYS_DEV = NB * TOK
KEYS_PAD = KEYS_DEV + 128
COUNT_IN = float(KEYS * (C_IN // GROUPS))
COUNT_MID = float(KEYS * (C // GROUPS))
BLK = 48
HALF = C_IN // 2
KEYS_DEV = NB * TOK
KEYS_PAD = KEYS_DEV + 128
COUNT_IN = float(KEYS * (C_IN // GROUPS))
COUNT_MID = float(KEYS * (C // GROUPS))
BLK = 48
HALF = C_IN // 2
KEYS_DEV = NB * TOK
KEYS_PAD = KEYS_DEV + 128
COUNT_IN = float(KEYS * (C_IN // GROUPS))
COUNT_MID = float(KEYS * (C // GROUPS))
BLK = 48
HALF = C_IN // 2
KEYS_DEV = NB * TOK
KEYS_PAD = KEYS_DEV + 128
PACK = KEYS_DEV // NA
RELAY = PACK + 3 * TOK
A = ("p", "x")
HIGH = lax.Precision.HIGHEST
NT = (((1,), (1,)), ((), ()))
VMEM_LIMIT = 20 * 1024 * 1024


def iota(shape, dim):
    return lax.broadcasted_iota(jnp.int32, shape, dim)


def pieces(row):
    hi = row.astype(BF16).astype(F32)
    mid = (row - hi).astype(BF16).astype(F32)
    lo = (row - hi - mid).astype(BF16).astype(F32)
    return hi, mid, lo


def fold_sums(rows, select):
    wide = jnp.dot(rows, select, precision=HIGH, preferred_element_type=F32)
    keep = (iota((8, 128), 1) >> 5) == iota((8, 128), 0)
    return jnp.sum(jnp.where(keep, wide, 0.0), axis=0, keepdims=True)


def spread_sums(line, select):
    keep = (iota((8, 128), 1) >> 5) == iota((8, 128), 0)
    rows = jnp.where(keep, jnp.broadcast_to(line, (8, 128)), 0.0)
    return jnp.dot(rows, select, precision=HIGH, preferred_element_type=F32)


def in_select(shape, group_dim, channel_dim):
    group = iota(shape, group_dim) & 31
    channel = iota(shape, channel_dim)
    return ((channel >= 10 * group) & (channel < 10 * group + 10)).astype(F32)


def slab_select(shape, x, dtype):
    row = iota(shape, 0)
    target = 40 * (row & 15) + 5 * x + (row >> 4)
    return (target == iota(shape, 1)).astype(dtype)


def pack_kernel_body(idx_ref, x1_ref, x2_ref, ker_ref, out_ref, rows_ref, lanes_ref):
    core = idx_ref[2]
    for t in range(9):
        both = ker_ref[t].astype(F32)
        rows_ref[5 * t : 5 * t + 5, :] = jnp.where(core == 0, both[:, :HALF], both[:, HALF:])
    x1 = x1_ref[...].astype(F32)
    x2 = x2_ref[...].astype(F32)
    sums = [jnp.sum(v, axis=0, keepdims=True) for v in (x1, x1 * x1, x2, x2 * x2)]
    sums = jnp.concatenate(sums + [jnp.zeros((4, C_IN), F32)], axis=0)
    line = fold_sums(sums, in_select((C_IN, 128), 1, 0))
    thirds = [rows_ref[15 * b : 15 * b + 15, :] for b in range(3)]
    lanes_ref[0:15, :] = jnp.concatenate(thirds + [jnp.zeros((15, 32), F32)], axis=1)
    lanes_ref[15:16, :] = jnp.concatenate(list(pieces(line)) + [jnp.zeros((1, 128), F32)], axis=1)
    block = lanes_ref[...].astype(BF16)

    def put(i, carry):
        out_ref[i] = block
        return carry

    lax.fori_loop(0, NB, put, 0)


def tokens_body(part_ref, x1_ref, x2_ref, halo_ref, after_ref, out_ref, again_ref):
    again_ref[...] = part_ref[...]
    part = jnp.sum(part_ref[:, :, 0:384].astype(F32), axis=0)[15:16]
    hi, mid, lo = pieces(part[:, 0:128] + part[:, 128:256] + part[:, 256:384])
    stats = jnp.concatenate([hi, mid, lo, jnp.zeros((5, 128), F32)], axis=0)
    stats = jnp.concatenate([stats, jnp.zeros((8, C_IN - 128), F32)], axis=1)
    tail = jnp.concatenate([halo_ref[...].astype(F32), stats], axis=0).astype(BF16)
    for i in range(NA):
        out_ref[i, 0:16, :] = x1_ref[...]
        out_ref[i, 16:32, :] = x2_ref[...]
        out_ref[i, 32:48, :] = tail


def slabs_body(idx_ref, feats_ref, tw_ref, sw_ref, sk_ref, tm_ref):
    mine = slab_select((CX, C), idx_ref[1], F32)
    time = jnp.dot(feats_ref[...], tw_ref[...].astype(F32), precision=HIGH, preferred_element_type=F32)
    tm_ref[...] = lax.dot_general(time, mine, NT, precision=HIGH, preferred_element_type=F32)
    sk_ref[...] = lax.dot_general(sw_ref[...], mine.astype(BF16), NT, preferred_element_type=F32).astype(BF16)


def weights_body(qw_ref, kw_ref, vw_ref, gm_ref, sm_ref, after_ref, w_ref, gs_ref, order_ref):
    row = iota((C, 1), 0)
    owner = jnp.zeros((C, 1), jnp.int32)
    for i in range(1, NA):
        owner = jnp.where(row >= CX * i, i, owner)
    row = row - CX * owner
    target = 40 * (row & 15) + 5 * owner + (row >> 4)
    order = jnp.where(target == iota((C, C), 1), 1.0, 0.0).astype(BF16)
    w_ref[...] = jnp.zeros(w_ref.shape, BF16)
    for n, ref in enumerate((qw_ref, kw_ref, vw_ref)):
        part = lax.dot_general(order, ref[...], NT, preferred_element_type=F32)
        w_ref[:, 384 * n : 384 * n + ATT] = part.astype(BF16)
    both = pieces(jnp.concatenate([gm_ref[...], sm_ref[...], jnp.zeros((6, C), F32)], axis=0))
    both = jnp.concatenate(list(both) + [jnp.zeros((8, C), F32)], axis=0).astype(BF16)
    both = lax.dot_general(both, order, NT, preferred_element_type=F32)
    gs_ref[...] = both[0:8] + both[8:16] + both[16:24]
    order_ref[...] = order


def conv_body(idx_ref, ker_ref, far_ref, tok_ref, skip_ref, time_ref, gain_ref, shift_ref, send_ref, own_ref, mark_ref, ker_f32):
    b = idx_ref[0]
    core = idx_ref[2]
    for n, ref in enumerate((ker_ref, far_ref)):
        for strip in range(4):
            ker_f32[n, strip] = ref[:, :, 128 * strip : 128 * strip + 128].astype(F32).reshape(NB * TOK, 128)
    stats = jnp.zeros((1, 128), F32)
    for j in range(NA):
        stats = stats + jnp.sum(tok_ref[j, 32:48, 0:128].astype(F32)[8:11], axis=0, keepdims=True)
    wide = spread_sums(stats, in_select((128, C_IN), 0, 1)) / COUNT_IN
    gain = gain_ref[...]
    shift = shift_ref[...]

    def act(values, s):
        mean = wide[2 * s : 2 * s + 1]
        spread = wide[2 * s + 1 : 2 * s + 2] - mean * mean
        n = (values - mean) * lax.rsqrt(spread + EPS) * gain + shift
        n = n / (1.0 + jnp.exp(-n))
        return n.astype(BF16).astype(F32)

    x1 = jnp.concatenate([tok_ref[j, 0:16, :] for j in range(NA)], axis=0)
    x2 = jnp.concatenate([tok_ref[j, 16:32, :] for j in range(NA)], axis=0)
    top = tok_ref[0, 32:48, :].astype(F32)[0:8]
    bottom = tok_ref[NA - 1, 32:48, :].astype(F32)[0:8]
    a1 = act(x1.astype(F32), 0)
    a2 = act(x2.astype(F32), 1)
    top = jnp.where(b == 0, 0.0, act(top, 0))
    bottom = jnp.where(b == NB - 1, 0.0, act(bottom, 0))
    a1 = jnp.concatenate([top, a1, bottom], axis=0)

    def near_first(a):
        swapped = jnp.concatenate([a[:, HALF:], a[:, :HALF]], axis=1)
        return jnp.where(core == 0, a, swapped)

    a1 = near_first(a1)
    a2 = near_first(a2)

    def columns(a):
        n = a.shape[0]
        col = iota(a.shape, 0) & 7
        left = jnp.where(col == 0, 0.0, pltpu.roll(a, 1, 0))
        right = jnp.where(col == 7, 0.0, pltpu.roll(a, n - 1, 0))
        return (left, a, right)

    cols1 = columns(a1)
    cols2 = columns(a2)
    rows = 2 * NA
    acc = jnp.dot(jnp.concatenate([x1, x2], axis=0), skip_ref[...], preferred_element_type=F32)
    conv = jnp.zeros((2 * NA * TOK, CX), F32)
    for dy in range(3):
        for dx in range(3):
            b1, b2 = cols1[dx], cols2[dx]
            first = b1[8 * dy : 8 * dy + 8 * rows]
            tiles = []
            for r in range(rows):
                stale = (dy == 0 and r % 2 == 0) or (dy == 2 and r % 2 == 1)
                at = r + dy - 1
                tiles.append(b1[8 * at + 8 : 8 * at + 16] if stale else b2[8 * at : 8 * at + 8])
            taps = jnp.concatenate([first] + tiles, axis=0).astype(BF16)
            t = 3 * dy + dx
            slab = []
            for k in range(5):
                third, row = divmod(5 * t + k, 15)
                strip, off = divmod(HALF * third, 128)
                ends = []
                for n in range(2):
                    pair = [ker_f32[n, strip + e, pl.ds(row, NB, stride=TOK), :] for e in range(2)]
                    ends.append(jnp.concatenate(pair, axis=1)[:, off : off + HALF])
                slab.append(jnp.concatenate(ends, axis=1))
            slab = jnp.concatenate(slab, axis=0).astype(BF16)
            conv = conv + lax.dot_general(taps, slab, NT, preferred_element_type=F32)
    half = NA * TOK
    step = iota((2 * half, 1), 0) >= half
    h = acc + conv + jnp.where(step, time_ref[1:2, :], time_ref[0:1, :])
    h = h.astype(BF16).astype(F32)
    h1 = h[:half]
    h2 = h[half:]
    sums = [jnp.sum(v, axis=0, keepdims=True) for v in (h1, h1 * h1, h2, h2 * h2)]
    sums = jnp.concatenate(sums + [jnp.zeros((4, CX), F32)], axis=0)
    group = 2 * (iota((CX, GROUPS), 0) & 15) + (idx_ref[1] >> 2)
    select = (group == iota((CX, GROUPS), 1)).astype(F32)
    sums = jnp.dot(sums, select, precision=HIGH, preferred_element_type=F32)
    side = jnp.concatenate([p[0:4] for p in pieces(sums)] + [jnp.zeros((4, GROUPS), F32)], axis=0)
    rest = jnp.zeros((TOK, 128 - CX - GROUPS), F32)
    blocks = [jnp.concatenate([h1[TOK * j : TOK * j + TOK], side, rest], axis=1).astype(BF16) for j in range(NA)]

    def put(i, carry):
        for j in range(NA):
            send_ref[NA * i + j] = blocks[j]
        return carry

    lax.fori_loop(0, NB, put, 0)
    both = [jnp.concatenate([v[TOK * j : TOK * j + TOK] for j in range(NA)], axis=1) for v in (h1, h2)]
    own_ref[...] = jnp.concatenate(both, axis=0).astype(BF16)
    mark_ref[...] = wide[:, 0:128]


def group_body(idx_ref, h_ref, order_ref, rows_ref, base_ref):
    for j in range(NA):
        parts = [h_ref[i, :, CX * j : CX * j + CX] for i in range(NA)]
        rows_ref[2 * TOK * j : 2 * TOK * j + 2 * TOK, :] = jnp.concatenate(parts, axis=1)
    own = pl.multiple_of(2 * TOK * idx_ref[1], 2 * TOK)
    base_ref[...] = jnp.dot(rows_ref[pl.ds(own, 2 * TOK), :], order_ref[...], preferred_element_type=F32)


def attend_body(idx_ref, h_ref, rows_ref, w_ref, gs_ref, send_ref, kk_ref, vv_ref, mq_ref):
    b = idx_ref[0]
    x = idx_ref[1]
    sums = jnp.sum(h_ref[...].astype(F32), axis=0)[:, CX : CX + GROUPS]
    sums = jnp.concatenate([sums[0:4] + sums[4:8] + sums[8:12], jnp.zeros((4, GROUPS), F32)], axis=0)
    lane = iota((GROUPS, C), 1)
    group = 2 * (lane & 15) + (lane >= C // 2).astype(jnp.int32)
    select = (group == iota((GROUPS, C), 0)).astype(F32)
    wide = jnp.dot(sums, select, precision=HIGH, preferred_element_type=F32) / COUNT_MID
    mean1, mean2 = wide[0:1], wide[2:3]
    rstd1 = lax.rsqrt(wide[1:2] - mean1 * mean1 + EPS)
    rstd2 = lax.rsqrt(wide[3:4] - mean2 * mean2 + EPS)
    gain = gs_ref[0:1, :]
    shift = gs_ref[1:2, :]

    def norm(h, mean, rstd):
        return (((h.astype(F32) - mean) * rstd) * gain + shift).astype(BF16)

    keys = []
    for n in range(NB):
        parts = [h_ref[NA * n + i, :, 0:CX] for i in range(NA)]
        keys.append(norm(jnp.concatenate(parts, axis=1), mean1, rstd1))
    keys = jnp.concatenate(keys, axis=0)
    second = ((iota((NA * 2 * TOK, 1), 0) >> 4) & 1) == 1
    mq_ref[...] = norm(rows_ref[...], jnp.where(second, mean2, mean1), jnp.where(second, rstd2, rstd1))
    keys = jnp.dot(keys, w_ref[:, 384:1152], preferred_element_type=F32)
    queries = jnp.dot(mq_ref[...], w_ref[:, 0:384], preferred_element_type=F32)
    own = pl.multiple_of(2 * TOK * x + TOK, TOK)
    fresh = jnp.dot(mq_ref[pl.ds(own, TOK), :], w_ref[:, 384:1152], preferred_element_type=F32)
    kk_ref[0:KEYS_DEV, :] = keys[:, 0:ATT].astype(BF16)
    vv_ref[0:KEYS_DEV, :] = keys[:, 384 : 384 + ATT].astype(BF16)
    kk_ref[KEYS_DEV : KEYS_DEV + TOK, :] = fresh[:, 0:ATT].astype(BF16)
    vv_ref[KEYS_DEV : KEYS_DEV + TOK, :] = fresh[:, 384 : 384 + ATT].astype(BF16)
    kk_ref[KEYS_DEV + TOK :, :] = jnp.zeros((KEYS_PAD - KEYS_DEV - TOK, ATT), BF16)
    vv_ref[KEYS_DEV + TOK :, :] = jnp.zeros((KEYS_PAD - KEYS_DEV - TOK, ATT), BF16)
    each = NA * 2 * TOK
    rows = HEADS * each
    q = queries[:, 0:ATT].astype(BF16).astype(F32) * (1.0 / math.sqrt(HEAD))
    lane_head = iota((each, ATT), 1) >> 6
    q = jnp.concatenate([jnp.where(lane_head == n, q, 0.0) for n in range(HEADS)], axis=0).astype(BF16)
    scores = lax.dot_general(q, kk_ref[...], NT, preferred_element_type=F32)
    col = iota((1, KEYS_PAD), 1)
    row = iota((rows, 1), 0)
    later = (((row >> 4) & 1) == 1) & (((row >> 5) & (NA - 1)) == x)
    low = b * TOK
    stale = (col >= low) & (col < low + TOK)
    usual = jnp.where(col < KEYS_DEV, 0.0, -1e30)
    special = jnp.where(stale | (col >= KEYS_DEV + TOK), -1e30, 0.0)
    scores = scores + jnp.where(later, special, usual)
    top = jnp.max(scores, axis=1, keepdims=True)
    weights = jnp.exp(scores - top)
    denom = jnp.sum(weights, axis=1, keepdims=True)
    mixed = jnp.dot(weights.astype(BF16), vv_ref[...], preferred_element_type=F32)
    out = jnp.zeros((each, ATT), F32)
    side = jnp.zeros((each, HEAD), F32)
    place = iota((each, HEAD), 1)
    split = pieces(top) + pieces(denom)
    for n in range(HEADS):
        at = slice(each * n, each * n + each)
        out = jnp.where(lane_head == n, mixed[at], out)
        for p in range(6):
            side = jnp.where(place == 8 * p + n, split[p][at], side)
    out = jnp.concatenate([out, side], axis=1).astype(BF16)
    for j in range(NA):
        send_ref[j] = out[2 * TOK * j : 2 * TOK * j + 2 * TOK]


def combine_body(part_ref, base_ref, ow_ref, o1_ref, o2_ref):
    sides = part_ref[:, :, ATT:].reshape(NA * 2 * TOK, HEAD)
    place = iota((HEAD, ATT), 0)
    same = (place & 7) == (iota((HEAD, ATT), 1) >> 6)
    tops = jnp.dot(sides, (same & (place < 24)).astype(BF16), preferred_element_type=F32)
    denoms = jnp.dot(sides, (same & (place >= 24) & (place < 48)).astype(BF16), preferred_element_type=F32)

    def of(values, i):
        return values[2 * TOK * i : 2 * TOK * i + 2 * TOK]

    top = of(tops, 0)
    for i in range(1, NA):
        top = jnp.maximum(top, of(tops, i))
    mixed = jnp.zeros((2 * TOK, ATT), F32)
    denom = jnp.zeros((2 * TOK, ATT), F32)
    for i in range(NA):
        factor = jnp.exp(of(tops, i) - top)
        mixed = mixed + part_ref[i, :, 0:ATT].astype(F32) * factor
        denom = denom + of(denoms, i) * factor
    out = (mixed / denom).astype(BF16)
    result = base_ref[...] + jnp.dot(out, ow_ref[...], preferred_element_type=F32)
    result = result.astype(BF16)
    o1_ref[...] = result[0:TOK]
    o2_ref[...] = result[TOK:]


def call(body, out_shape, in_specs, scratch=(), cost=None):
    many = isinstance(out_shape, (list, tuple))
    vmem = pl.BlockSpec(memory_space=pltpu.VMEM)
    return pl.pallas_call(
        body,
        out_shape=out_shape,
        in_specs=in_specs,
        out_specs=[vmem] * len(out_shape) if many else vmem,
        scratch_shapes=list(scratch),
        compiler_params=pltpu.CompilerParams(vmem_limit_bytes=VMEM_LIMIT),
        cost_estimate=cost,
    )


def shape(dims, dtype=BF16):
    return jax.ShapeDtypeStruct(dims, dtype)


def spread(blocks, axis):
    return lax.all_to_all(blocks, axis, 0, 0, tiled=True)


def time_features(steps_int, width):
    half = width // 2
    freqs = jnp.exp(-math.log(10000.0) * jnp.arange(half, dtype=F32) / half)
    angles = steps_int.astype(F32)[:, None] * freqs[None, :]
    return jnp.concatenate([jnp.cos(angles), jnp.sin(angles)], axis=1)


def per_device(
    x_first,
    x_second,
    timesteps,
    conv_kernel,
    skip_weight,
    time_weight,
    gain_in,
    shift_in,
    gain_mid,
    shift_mid,
    query_weight,
    key_weight,
    value_weight,
    out_weight,
):
    vmem = pl.BlockSpec(memory_space=pltpu.VMEM)
    smem = pl.BlockSpec(memory_space=pltpu.SMEM)
    b = lax.axis_index("b")
    x = lax.axis_index(A)
    idx = jnp.stack([b, x, lax.axis_index("core")]).astype(jnp.int32)
    x1 = x_first.reshape(TOK, C_IN)
    x2 = x_second.reshape(TOK, C_IN)

    whole = lambda *dims: pl.BlockSpec(dims, lambda i: (0,) * len(dims))
    first = pl.pallas_call(
        pack_kernel_body,
        grid=(1,),
        out_shape=shape((NB, TOK, 512)),
        in_specs=[smem, whole(TOK, C_IN), whole(TOK, C_IN), whole(9, 5, C_IN)],
        out_specs=whole(NB, TOK, 512),
        scratch_shapes=[pltpu.VMEM((BLK, HALF), F32), pltpu.VMEM((TOK, 512), F32)],
        compiler_params=pltpu.CompilerParams(vmem_limit_bytes=VMEM_LIMIT),
    )(idx, x1, x2, jnp.transpose(conv_kernel, (1, 0, 2)))
    edge = jnp.where(x == NA - 1, x_first[1], x_first[0])
    pairs = []
    for g in range(NB - 1):
        pairs += [(NA * g + NA - 1, NA * g + NA), (NA * g + NA, NA * g + NA - 1)]
    halo = lax.ppermute(edge, ("b",) + A, pairs)
    kernels = spread(first, "b")

    feats = jax.nn.silu(time_features(timesteps, C_IN))
    feats = jnp.pad(feats, ((0, 6), (0, 0)))
    skip_slab, time_slab = call(
        slabs_body,
        [shape((C_IN, CX)), shape((8, CX), F32)],
        [smem] + [vmem] * 3,
        cost=pl.CostEstimate(flops=2 * 640 * 320 * 200, bytes_accessed=1 << 20, transcendentals=0),
    )(idx, feats, time_weight, skip_weight)

    tokens, again = call(tokens_body, [shape((NA, BLK, C_IN)), shape((NB, TOK, 512))], [vmem] * 5)(
        kernels, x1, x2, halo, time_slab
    )
    far = lax.ppermute(again, "core", [(0, 1), (1, 0)])
    tokens = spread(tokens, A)

    send, own, mark = call(
        conv_body,
        [shape((NB * NA, TOK, 128)), shape((2 * TOK, C)), shape((8, 128), F32)],
        [smem] + [vmem] * 7,
        [pltpu.VMEM((2, 4, NB * TOK, 128), F32)],
    )(idx, kernels, far, tokens, skip_slab, time_slab, gain_in[None], shift_in[None])
    everyone = spread(send, ("b",) + A)
    group = lax.all_gather(own, "x", axis=0, tiled=True)
    group = lax.all_gather(group, "p", axis=0, tiled=True).reshape(NA, 2 * TOK, C)
    weights, scale_mid, order = call(
        weights_body,
        [shape((C, 1152)), shape((8, C), F32), shape((C, C))],
        [vmem] * 6,
        cost=pl.CostEstimate(flops=2 * 640 * 640 * 1200, bytes_accessed=4 << 20, transcendentals=0),
    )(query_weight.T, key_weight.T, value_weight.T, gain_mid[None], shift_mid[None], mark)
    rows, base = call(group_body, [shape((NA * 2 * TOK, C)), shape((2 * TOK, C), F32)], [smem] + [vmem] * 2)(idx, group, order)
    partial = call(
        attend_body,
        shape((NA, 2 * TOK, ATT + HEAD)),
        [smem] + [vmem] * 4,
        [pltpu.VMEM((KEYS_PAD, ATT), BF16), pltpu.VMEM((KEYS_PAD, ATT), BF16), pltpu.VMEM((NA * 2 * TOK, C), BF16)],
    )(idx, everyone, rows, weights, scale_mid)
    partial = spread(partial, A)
    out1, out2 = call(combine_body, [shape((TOK, C)), shape((TOK, C))], [vmem] * 3)(partial, base, out_weight)
    dims = x_first.shape[:2] + (C,)
    return out1.reshape(dims), out2.reshape(dims)


def solution(mesh):
    grid = Mesh(mesh.devices.reshape(NB, 2, NA // 2, 2, 2), ("b", "p", "x", "y_hi", "core"))
    tokens = P(("y_hi", "core", "b", "p", "x"), None, None)
    return jax.shard_map(
        per_device,
        mesh=grid,
        in_specs=(tokens, tokens, P(), P(("b", "p", "x"), None, None)) + (P(),) * 10,
        out_specs=(tokens, tokens),
        check_vma=False,
    )
```

```python
import functools
import math

import jax
import jax.numpy as jnp
from jax import lax
from jax.experimental import pallas as pl
from jax.experimental.pallas import tpu as pltpu
from jax.sharding import Mesh, PartitionSpec as P

F32 = jnp.float32
BF16 = jnp.bfloat16
HEADS = 5
HEAD = 64
GROUPS = 32
C_IN = 320
C = 640
ATT = HEADS * HEAD
EPS = 1e-05
NB = 16
NA = 8
TOK = 16
CX = C // NA
KEYS = NB * NA * TOK
COUNT_IN = float(KEYS * (C_IN // GROUPS))
COUNT_MID = float(KEYS * (C // GROUPS))
BLK = 48
HALF = C_IN // 2
KEYS_DEV = NB * TOK
KEYS_PAD = KEYS_DEV + 128
COUNT_IN = float(KEYS * (C_IN // GROUPS))
COUNT_MID = float(KEYS * (C // GROUPS))
BLK = 48
HALF = C_IN // 2
KEYS_DEV = NB * TOK
KEYS_PAD = KEYS_DEV + 128
COUNT_IN = float(KEYS * (C_IN // GROUPS))
COUNT_MID = float(KEYS * (C // GROUPS))
BLK = 48
HALF = C_IN // 2
KEYS_DEV = NB * TOK
KEYS_PAD = KEYS_DEV + 128
COUNT_IN = float(KEYS * (C_IN // GROUPS))
COUNT_MID = float(KEYS * (C // GROUPS))
BLK = 48
HALF = C_IN // 2
KEYS_DEV = NB * TOK
KEYS_PAD = KEYS_DEV + 128
PACK = KEYS_DEV // NA
RELAY = PACK + 3 * TOK
A = ("p", "x")
HIGH = lax.Precision.HIGHEST
NT = (((1,), (1,)), ((), ()))
VMEM_LIMIT = 20 * 1024 * 1024


def iota(shape, dim):
    return lax.broadcasted_iota(jnp.int32, shape, dim)


def pieces(row):
    hi = row.astype(BF16).astype(F32)
    mid = (row - hi).astype(BF16).astype(F32)
    lo = (row - hi - mid).astype(BF16).astype(F32)
    return hi, mid, lo


def fold_sums(rows, select):
    wide = jnp.dot(rows, select, precision=HIGH, preferred_element_type=F32)
    keep = (iota((8, 128), 1) >> 5) == iota((8, 128), 0)
    return jnp.sum(jnp.where(keep, wide, 0.0), axis=0, keepdims=True)


def spread_sums(line, select):
    keep = (iota((8, 128), 1) >> 5) == iota((8, 128), 0)
    rows = jnp.where(keep, jnp.broadcast_to(line, (8, 128)), 0.0)
    return jnp.dot(rows, select, precision=HIGH, preferred_element_type=F32)


def in_select(shape, group_dim, channel_dim):
    group = iota(shape, group_dim) & 31
    channel = iota(shape, channel_dim)
    return ((channel >= 10 * group) & (channel < 10 * group + 10)).astype(F32)


def slab_select(shape, x, dtype):
    row = iota(shape, 0)
    target = 40 * (row & 15) + 5 * x + (row >> 4)
    return (target == iota(shape, 1)).astype(dtype)


def pack_kernel_body(idx_ref, x1_ref, x2_ref, ker_ref, out_ref, edge_ref, rows_ref, lanes_ref):
    core = idx_ref[2]
    for t in range(9):
        both = ker_ref[t].astype(F32)
        rows_ref[5 * t : 5 * t + 5, :] = jnp.where(core == 0, both[:, :HALF], both[:, HALF:])
    x1 = x1_ref[...].astype(F32)
    x2 = x2_ref[...].astype(F32)
    edge_ref[...] = jnp.where(idx_ref[1] == NA - 1, x1[8:16], x1[0:8]).astype(BF16)
    sums = [jnp.sum(v, axis=0, keepdims=True) for v in (x1, x1 * x1, x2, x2 * x2)]
    sums = jnp.concatenate(sums + [jnp.zeros((4, C_IN), F32)], axis=0)
    line = fold_sums(sums, in_select((C_IN, 128), 1, 0))
    thirds = [rows_ref[15 * b : 15 * b + 15, :] for b in range(3)]
    lanes_ref[0:15, :] = jnp.concatenate(thirds + [jnp.zeros((15, 32), F32)], axis=1)
    lanes_ref[15:16, :] = jnp.concatenate(list(pieces(line)) + [jnp.zeros((1, 128), F32)], axis=1)
    block = lanes_ref[...].astype(BF16)

    def put(i, carry):
        out_ref[i] = block
        return carry

    lax.fori_loop(0, NB, put, 0)


def tokens_body(part_ref, x1_ref, x2_ref, halo_ref, after_ref, out_ref, again_ref):
    again_ref[...] = part_ref[...]
    part = jnp.sum(part_ref[:, :, 0:384].astype(F32), axis=0)[15:16]
    hi, mid, lo = pieces(part[:, 0:128] + part[:, 128:256] + part[:, 256:384])
    stats = jnp.concatenate([hi, mid, lo, jnp.zeros((5, 128), F32)], axis=0)
    stats = jnp.concatenate([stats, jnp.zeros((8, C_IN - 128), F32)], axis=1)
    tail = jnp.concatenate([halo_ref[...].astype(F32), stats], axis=0).astype(BF16)
    for i in range(NA):
        out_ref[i, 0:16, :] = x1_ref[...]
        out_ref[i, 16:32, :] = x2_ref[...]
        out_ref[i, 32:48, :] = tail


def slabs_body(idx_ref, feats_ref, tw_ref, sw_ref, sk_ref, tm_ref):
    mine = slab_select((CX, C), idx_ref[1], F32)
    time = jnp.dot(feats_ref[...], tw_ref[...].astype(F32), precision=HIGH, preferred_element_type=F32)
    tm_ref[...] = lax.dot_general(time, mine, NT, precision=HIGH, preferred_element_type=F32)
    sk_ref[...] = lax.dot_general(sw_ref[...], mine.astype(BF16), NT, preferred_element_type=F32).astype(BF16)


def order_select():
    row = iota((C, 1), 0)
    owner = jnp.zeros((C, 1), jnp.int32)
    for i in range(1, NA):
        owner = jnp.where(row >= CX * i, i, owner)
    row = row - CX * owner
    target = 40 * (row & 15) + 5 * owner + (row >> 4)
    return jnp.where(target == iota((C, C), 1), 1.0, 0.0).astype(BF16)


def conv_body(idx_ref, ker_ref, far_ref, tok_ref, skip_ref, time_ref, gain_ref, shift_ref, send_ref, own_ref, ker_f32):
    b = idx_ref[0]
    core = idx_ref[2]
    for n, ref in enumerate((ker_ref, far_ref)):
        for strip in range(4):
            ker_f32[n, strip] = ref[:, :, 128 * strip : 128 * strip + 128].astype(F32).reshape(NB * TOK, 128)
    stats = jnp.zeros((1, 128), F32)
    for j in range(NA):
        stats = stats + jnp.sum(tok_ref[j, 32:48, 0:128].astype(F32)[8:11], axis=0, keepdims=True)
    wide = spread_sums(stats, in_select((128, C_IN), 0, 1)) / COUNT_IN
    gain = gain_ref[...]
    shift = shift_ref[...]

    def act(values, s):
        mean = wide[2 * s : 2 * s + 1]
        spread = wide[2 * s + 1 : 2 * s + 2] - mean * mean
        n = (values - mean) * lax.rsqrt(spread + EPS) * gain + shift
        n = n / (1.0 + jnp.exp(-n))
        return n.astype(BF16).astype(F32)

    x1 = jnp.concatenate([tok_ref[j, 0:16, :] for j in range(NA)], axis=0)
    x2 = jnp.concatenate([tok_ref[j, 16:32, :] for j in range(NA)], axis=0)
    top = tok_ref[0, 32:48, :].astype(F32)[0:8]
    bottom = tok_ref[NA - 1, 32:48, :].astype(F32)[0:8]
    a1 = act(x1.astype(F32), 0)
    a2 = act(x2.astype(F32), 1)
    top = jnp.where(b == 0, 0.0, act(top, 0))
    bottom = jnp.where(b == NB - 1, 0.0, act(bottom, 0))
    a1 = jnp.concatenate([top, a1, bottom], axis=0)

    def near_first(a):
        swapped = jnp.concatenate([a[:, HALF:], a[:, :HALF]], axis=1)
        return jnp.where(core == 0, a, swapped)

    a1 = near_first(a1)
    a2 = near_first(a2)

    def columns(a):
        n = a.shape[0]
        col = iota(a.shape, 0) & 7
        left = jnp.where(col == 0, 0.0, pltpu.roll(a, 1, 0))
        right = jnp.where(col == 7, 0.0, pltpu.roll(a, n - 1, 0))
        return (left, a, right)

    cols1 = columns(a1)
    cols2 = columns(a2)
    rows = 2 * NA
    acc = jnp.dot(jnp.concatenate([x1, x2], axis=0), skip_ref[...], preferred_element_type=F32)
    conv = jnp.zeros((2 * NA * TOK, CX), F32)
    for dy in range(3):
        for dx in range(3):
            b1, b2 = cols1[dx], cols2[dx]
            first = b1[8 * dy : 8 * dy + 8 * rows]
            tiles = []
            for r in range(rows):
                stale = (dy == 0 and r % 2 == 0) or (dy == 2 and r % 2 == 1)
                at = r + dy - 1
                tiles.append(b1[8 * at + 8 : 8 * at + 16] if stale else b2[8 * at : 8 * at + 8])
            taps = jnp.concatenate([first] + tiles, axis=0).astype(BF16)
            t = 3 * dy + dx
            slab = []
            for k in range(5):
                third, row = divmod(5 * t + k, 15)
                strip, off = divmod(HALF * third, 128)
                ends = []
                for n in range(2):
                    pair = [ker_f32[n, strip + e, pl.ds(row, NB, stride=TOK), :] for e in range(2)]
                    ends.append(jnp.concatenate(pair, axis=1)[:, off : off + HALF])
                slab.append(jnp.concatenate(ends, axis=1))
            slab = jnp.concatenate(slab, axis=0).astype(BF16)
            conv = conv + lax.dot_general(taps, slab, NT, preferred_element_type=F32)
    half = NA * TOK
    step = iota((2 * half, 1), 0) >= half
    h = acc + conv + jnp.where(step, time_ref[1:2, :], time_ref[0:1, :])
    h = h.astype(BF16).astype(F32)
    h1 = h[:half]
    h2 = h[half:]
    sums = [jnp.sum(v, axis=0, keepdims=True) for v in (h1, h1 * h1, h2, h2 * h2)]
    sums = jnp.concatenate(sums + [jnp.zeros((4, CX), F32)], axis=0)
    group = 2 * (iota((CX, GROUPS), 0) & 15) + (idx_ref[1] >> 2)
    select = (group == iota((CX, GROUPS), 1)).astype(F32)
    sums = jnp.dot(sums, select, precision=HIGH, preferred_element_type=F32)
    side = jnp.concatenate([p[0:4] for p in pieces(sums)] + [jnp.zeros((4, GROUPS), F32)], axis=0)
    rest = jnp.zeros((TOK, 128 - CX - GROUPS), F32)
    blocks = [jnp.concatenate([h1[TOK * j : TOK * j + TOK], side, rest], axis=1).astype(BF16) for j in range(NA)]

    def put(i, carry):
        for j in range(NA):
            send_ref[NA * i + j] = blocks[j]
        return carry

    lax.fori_loop(0, NB, put, 0)
    both = [jnp.concatenate([v[TOK * j : TOK * j + TOK] for j in range(NA)], axis=1) for v in (h1, h2)]
    own_ref[...] = jnp.concatenate(both, axis=0).astype(BF16)


def group_body(idx_ref, h_ref, rows_ref, base_ref):
    order = order_select()
    blocks = [h_ref[i] for i in range(NA)]
    rows = []
    for j in range(NA):
        rows.append(jnp.concatenate([block[:, CX * j : CX * j + CX] for block in blocks], axis=1))
    rows = jnp.concatenate(rows, axis=0)
    rows_ref[...] = jnp.dot(rows, order, preferred_element_type=F32).astype(BF16)
    own = pl.multiple_of(2 * TOK * idx_ref[1], 2 * TOK)
    base_ref[...] = rows_ref[pl.ds(own, 2 * TOK), :].astype(F32)


def attend_body(idx_ref, h_ref, rows_ref, qw_ref, kw_ref, vw_ref, gain_ref, shift_ref, send_ref, kk_ref, vv_ref, mq_ref):
    b = idx_ref[0]
    x = idx_ref[1]
    sums = jnp.sum(h_ref[...].astype(F32), axis=0)[:, CX : CX + GROUPS]
    sums = jnp.concatenate([sums[0:4] + sums[4:8] + sums[8:12], jnp.zeros((4, GROUPS), F32)], axis=0)
    group = 20 * iota((GROUPS, C), 0)
    channel = iota((GROUPS, C), 1)
    select = ((channel >= group) & (channel < group + 20)).astype(F32)
    wide = jnp.dot(sums, select, precision=HIGH, preferred_element_type=F32) / COUNT_MID
    mean1, mean2 = wide[0:1], wide[2:3]
    rstd1 = lax.rsqrt(wide[1:2] - mean1 * mean1 + EPS)
    rstd2 = lax.rsqrt(wide[3:4] - mean2 * mean2 + EPS)
    gain = gain_ref[...]
    shift = shift_ref[...]

    def norm(h, mean, rstd):
        return (((h - mean) * rstd) * gain + shift).astype(BF16)

    def project(m, ref):
        return lax.dot_general(m, ref[...], NT, preferred_element_type=F32).astype(BF16)

    keys = []
    for n in range(NB):
        keys.append(jnp.concatenate([h_ref[NA * n + i, :, 0:CX] for i in range(NA)], axis=1))
    keys = jnp.concatenate(keys, axis=0)
    keys = norm(jnp.dot(keys, order_select(), preferred_element_type=F32), mean1, rstd1)
    second = ((iota((NA * 2 * TOK, 1), 0) >> 4) & 1) == 1
    mean = jnp.where(second, mean2, mean1)
    rstd = jnp.where(second, rstd2, rstd1)
    mq_ref[...] = norm(rows_ref[...].astype(F32), mean, rstd)
    queries = project(mq_ref[...], qw_ref)
    fresh = mq_ref[pl.ds(pl.multiple_of(2 * TOK * x + TOK, TOK), TOK), :]
    for ref, weight in ((kk_ref, kw_ref), (vv_ref, vw_ref)):
        ref[0:KEYS_DEV, :] = project(keys, weight)
        ref[KEYS_DEV : KEYS_DEV + TOK, :] = project(fresh, weight)
        ref[KEYS_DEV + TOK :, :] = jnp.zeros((KEYS_PAD - KEYS_DEV - TOK, ATT), BF16)
    each = NA * 2 * TOK
    rows = HEADS * each
    q = queries.astype(F32) * (1.0 / math.sqrt(HEAD))
    lane_head = iota((each, ATT), 1) >> 6
    q = jnp.concatenate([jnp.where(lane_head == n, q, 0.0) for n in range(HEADS)], axis=0).astype(BF16)
    scores = lax.dot_general(q, kk_ref[...], NT, preferred_element_type=F32)
    col = iota((1, KEYS_PAD), 1)
    row = iota((rows, 1), 0)
    later = (((row >> 4) & 1) == 1) & (((row >> 5) & (NA - 1)) == x)
    low = b * TOK
    stale = (col >= low) & (col < low + TOK)
    usual = jnp.where(col < KEYS_DEV, 0.0, -1e30)
    special = jnp.where(stale | (col >= KEYS_DEV + TOK), -1e30, 0.0)
    scores = scores + jnp.where(later, special, usual)
    top = jnp.max(scores, axis=1, keepdims=True)
    weights = jnp.exp(scores - top)
    denom = jnp.sum(weights, axis=1, keepdims=True)
    mixed = jnp.dot(weights.astype(BF16), vv_ref[...], preferred_element_type=F32)
    out = jnp.zeros((each, ATT), F32)
    side = jnp.zeros((each, HEAD), F32)
    place = iota((each, HEAD), 1)
    split = pieces(top) + pieces(denom)
    for n in range(HEADS):
        at = slice(each * n, each * n + each)
        out = jnp.where(lane_head == n, mixed[at], out)
        for p in range(6):
            side = jnp.where(place == 8 * p + n, split[p][at], side)
    out = jnp.concatenate([out, side], axis=1).astype(BF16)
    for j in range(NA):
        send_ref[j] = out[2 * TOK * j : 2 * TOK * j + 2 * TOK]


def combine_body(part_ref, base_ref, ow_ref, o1_ref, o2_ref):
    sides = part_ref[:, :, ATT:].reshape(NA * 2 * TOK, HEAD)
    place = iota((HEAD, ATT), 0)
    same = (place & 7) == (iota((HEAD, ATT), 1) >> 6)
    tops = jnp.dot(sides, (same & (place < 24)).astype(BF16), preferred_element_type=F32)
    denoms = jnp.dot(sides, (same & (place >= 24) & (place < 48)).astype(BF16), preferred_element_type=F32)

    def of(values, i):
        return values[2 * TOK * i : 2 * TOK * i + 2 * TOK]

    top = of(tops, 0)
    for i in range(1, NA):
        top = jnp.maximum(top, of(tops, i))
    mixed = jnp.zeros((2 * TOK, ATT), F32)
    denom = jnp.zeros((2 * TOK, ATT), F32)
    for i in range(NA):
        factor = jnp.exp(of(tops, i) - top)
        mixed = mixed + part_ref[i, :, 0:ATT].astype(F32) * factor
        denom = denom + of(denoms, i) * factor
    out = (mixed / denom).astype(BF16)
    result = base_ref[...] + jnp.dot(out, ow_ref[...], preferred_element_type=F32)
    result = result.astype(BF16)
    o1_ref[...] = result[0:TOK]
    o2_ref[...] = result[TOK:]


def call(body, out_shape, in_specs, scratch=(), cost=None):
    many = isinstance(out_shape, (list, tuple))
    vmem = pl.BlockSpec(memory_space=pltpu.VMEM)
    return pl.pallas_call(
        body,
        out_shape=out_shape,
        in_specs=in_specs,
        out_specs=[vmem] * len(out_shape) if many else vmem,
        scratch_shapes=list(scratch),
        compiler_params=pltpu.CompilerParams(vmem_limit_bytes=VMEM_LIMIT),
        cost_estimate=cost,
    )


def shape(dims, dtype=BF16):
    return jax.ShapeDtypeStruct(dims, dtype)


def spread(blocks, axis):
    return lax.all_to_all(blocks, axis, 0, 0, tiled=True)


def time_features(steps_int, width):
    half = width // 2
    freqs = jnp.exp(-math.log(10000.0) * jnp.arange(half, dtype=F32) / half)
    angles = steps_int.astype(F32)[:, None] * freqs[None, :]
    return jnp.concatenate([jnp.cos(angles), jnp.sin(angles)], axis=1)


def per_device(
    x_first,
    x_second,
    timesteps,
    conv_kernel,
    skip_weight,
    time_weight,
    gain_in,
    shift_in,
    gain_mid,
    shift_mid,
    query_weight,
    key_weight,
    value_weight,
    out_weight,
):
    vmem = pl.BlockSpec(memory_space=pltpu.VMEM)
    smem = pl.BlockSpec(memory_space=pltpu.SMEM)
    b = lax.axis_index("b")
    x = lax.axis_index(A)
    idx = jnp.stack([b, x, lax.axis_index("core")]).astype(jnp.int32)
    x1 = x_first.reshape(TOK, C_IN)
    x2 = x_second.reshape(TOK, C_IN)

    whole = lambda *dims: pl.BlockSpec(dims, lambda i: (0,) * len(dims))
    first, edge = pl.pallas_call(
        pack_kernel_body,
        grid=(1,),
        out_shape=[shape((NB, TOK, 512)), shape((8, C_IN))],
        in_specs=[smem, whole(TOK, C_IN), whole(TOK, C_IN), whole(9, 5, C_IN)],
        out_specs=[whole(NB, TOK, 512), whole(8, C_IN)],
        scratch_shapes=[pltpu.VMEM((BLK, HALF), F32), pltpu.VMEM((TOK, 512), F32)],
        compiler_params=pltpu.CompilerParams(vmem_limit_bytes=3 * VMEM_LIMIT),
    )(idx, x1, x2, jnp.transpose(conv_kernel, (1, 0, 2)))
    pairs = []
    for g in range(NB - 1):
        pairs += [(NA * g + NA - 1, NA * g + NA), (NA * g + NA, NA * g + NA - 1)]
    halo = lax.ppermute(edge, ("b",) + A, pairs)
    kernels = spread(first, "b")

    feats = jax.nn.silu(time_features(timesteps, C_IN))
    feats = jnp.pad(feats, ((0, 6), (0, 0)))
    skip_slab, time_slab = call(
        slabs_body,
        [shape((C_IN, CX)), shape((8, CX), F32)],
        [smem] + [vmem] * 3,
        cost=pl.CostEstimate(flops=2 * 640 * 320 * 200, bytes_accessed=1 << 20, transcendentals=0),
    )(idx, feats, time_weight, skip_weight)

    tokens, again = call(tokens_body, [shape((NA, BLK, C_IN)), shape((NB, TOK, 512))], [vmem] * 5)(
        kernels, x1, x2, halo, time_slab
    )
    far = lax.ppermute(again, "core", [(0, 1), (1, 0)])
    tokens = spread(tokens, A)

    send, own = call(
        conv_body,
        [shape((NB * NA, TOK, 128)), shape((2 * TOK, C))],
        [smem] + [vmem] * 7,
        [pltpu.VMEM((2, 4, NB * TOK, 128), F32)],
    )(idx, kernels, far, tokens, skip_slab, time_slab, gain_in[None], shift_in[None])
    everyone = spread(send, ("b",) + A)
    group = lax.all_gather(own, "x", axis=0, tiled=True)
    group = lax.all_gather(group, "p", axis=0, tiled=True)
    rows, base = call(group_body, [shape((NA * 2 * TOK, C)), shape((2 * TOK, C), F32)], [smem, vmem])(
        idx, group.reshape(NA, 2 * TOK, C)
    )
    partial = call(
        attend_body,
        shape((NA, 2 * TOK, ATT + HEAD)),
        [smem] + [vmem] * 7,
        [pltpu.VMEM((KEYS_PAD, ATT), BF16), pltpu.VMEM((KEYS_PAD, ATT), BF16), pltpu.VMEM((NA * 2 * TOK, C), BF16)],
    )(idx, everyone, rows, query_weight.T, key_weight.T, value_weight.T, gain_mid[None], shift_mid[None])
    partial = spread(partial, A)
    out1, out2 = call(combine_body, [shape((TOK, C)), shape((TOK, C))], [vmem] * 3)(partial, base, out_weight)
    dims = x_first.shape[:2] + (C,)
    return out1.reshape(dims), out2.reshape(dims)


def solution(mesh):
    grid = Mesh(mesh.devices.reshape(NB, 2, NA // 2, 2, 2), ("b", "p", "x", "y_hi", "core"))
    tokens = P(("y_hi", "core", "b", "p", "x"), None, None)
    return jax.shard_map(
        per_device,
        mesh=grid,
        in_specs=(tokens, tokens, P(), P(("b", "p", "x"), None, None)) + (P(),) * 10,
        out_specs=(tokens, tokens),
        check_vma=False,
    )
```

```python
import functools
import math

import jax
import jax.numpy as jnp
from jax import lax
from jax.experimental import pallas as pl
from jax.experimental.pallas import tpu as pltpu
from jax.sharding import Mesh, PartitionSpec as P

F32 = jnp.float32
BF16 = jnp.bfloat16
HEADS = 5
HEAD = 64
GROUPS = 32
C_IN = 320
C = 640
ATT = HEADS * HEAD
EPS = 1e-05
NB = 16
NA = 8
TOK = 16
CX = C // NA
KEYS = NB * NA * TOK
COUNT_IN = float(KEYS * (C_IN // GROUPS))
COUNT_MID = float(KEYS * (C // GROUPS))
BLK = 48
HALF = C_IN // 2
KEYS_DEV = NB * TOK
KEYS_PAD = KEYS_DEV + 128
COUNT_IN = float(KEYS * (C_IN // GROUPS))
COUNT_MID = float(KEYS * (C // GROUPS))
BLK = 48
HALF = C_IN // 2
KEYS_DEV = NB * TOK
KEYS_PAD = KEYS_DEV + 128
COUNT_IN = float(KEYS * (C_IN // GROUPS))
COUNT_MID = float(KEYS * (C // GROUPS))
BLK = 48
HALF = C_IN // 2
KEYS_DEV = NB * TOK
KEYS_PAD = KEYS_DEV + 128
COUNT_IN = float(KEYS * (C_IN // GROUPS))
COUNT_MID = float(KEYS * (C // GROUPS))
BLK = 48
HALF = C_IN // 2
KEYS_DEV = NB * TOK
KEYS_PAD = KEYS_DEV + 128
PACK = KEYS_DEV // NA
RELAY = PACK + 3 * TOK
A = ("p", "x")
HIGH = lax.Precision.HIGHEST
NT = (((1,), (1,)), ((), ()))
VMEM_LIMIT = 20 * 1024 * 1024


def iota(shape, dim):
    return lax.broadcasted_iota(jnp.int32, shape, dim)


def pieces(row):
    hi = row.astype(BF16).astype(F32)
    mid = (row - hi).astype(BF16).astype(F32)
    lo = (row - hi - mid).astype(BF16).astype(F32)
    return hi, mid, lo


def fold_sums(rows, select):
    wide = jnp.dot(rows, select, precision=HIGH, preferred_element_type=F32)
    keep = (iota((8, 128), 1) >> 5) == iota((8, 128), 0)
    return jnp.sum(jnp.where(keep, wide, 0.0), axis=0, keepdims=True)


def spread_sums(line, select):
    keep = (iota((8, 128), 1) >> 5) == iota((8, 128), 0)
    rows = jnp.where(keep, jnp.broadcast_to(line, (8, 128)), 0.0)
    return jnp.dot(rows, select, precision=HIGH, preferred_element_type=F32)


def in_select(shape, group_dim, channel_dim):
    group = iota(shape, group_dim) & 31
    channel = iota(shape, channel_dim)
    return ((channel >= 10 * group) & (channel < 10 * group + 10)).astype(F32)


def slab_select(shape, x, dtype):
    row = iota(shape, 0)
    target = 40 * (row & 15) + 5 * x + (row >> 4)
    return (target == iota(shape, 1)).astype(dtype)


def pack_kernel_body(idx_ref, x1_ref, x2_ref, ker_ref, out_ref, edge_ref, rows_ref, lanes_ref):
    core = idx_ref[2]
    for t in range(9):
        both = ker_ref[t].astype(F32)
        rows_ref[5 * t : 5 * t + 5, :] = jnp.where(core == 0, both[:, :HALF], both[:, HALF:])
    x1 = x1_ref[...].astype(F32)
    x2 = x2_ref[...].astype(F32)
    edge_ref[...] = jnp.where(idx_ref[1] == NA - 1, x1[8:16], x1[0:8]).astype(BF16)
    sums = [jnp.sum(v, axis=0, keepdims=True) for v in (x1, x1 * x1, x2, x2 * x2)]
    sums = jnp.concatenate(sums + [jnp.zeros((4, C_IN), F32)], axis=0)
    line = fold_sums(sums, in_select((C_IN, 128), 1, 0))
    thirds = [rows_ref[15 * b : 15 * b + 15, :] for b in range(3)]
    lanes_ref[0:15, :] = jnp.concatenate(thirds + [jnp.zeros((15, 32), F32)], axis=1)
    lanes_ref[15:16, :] = jnp.concatenate(list(pieces(line)) + [jnp.zeros((1, 128), F32)], axis=1)
    block = lanes_ref[...].astype(BF16)

    def put(i, carry):
        out_ref[i] = block
        return carry

    lax.fori_loop(0, NB, put, 0)


def tokens_body(part_ref, x1_ref, x2_ref, halo_ref, after_ref, out_ref, again_ref):
    again_ref[...] = part_ref[...]
    part = jnp.sum(part_ref[:, :, 0:384].astype(F32), axis=0)[15:16]
    hi, mid, lo = pieces(part[:, 0:128] + part[:, 128:256] + part[:, 256:384])
    stats = jnp.concatenate([hi, mid, lo, jnp.zeros((5, 128), F32)], axis=0)
    stats = jnp.concatenate([stats, jnp.zeros((8, C_IN - 128), F32)], axis=1)
    tail = jnp.concatenate([halo_ref[...].astype(F32), stats], axis=0).astype(BF16)
    for i in range(NA):
        out_ref[i, 0:16, :] = x1_ref[...]
        out_ref[i, 16:32, :] = x2_ref[...]
        out_ref[i, 32:48, :] = tail


def slabs_body(idx_ref, feats_ref, tw_ref, sw_ref, sk_ref, tm_ref):
    mine = slab_select((CX, C), idx_ref[1], F32)
    time = jnp.dot(feats_ref[...], tw_ref[...].astype(F32), precision=HIGH, preferred_element_type=F32)
    tm_ref[...] = lax.dot_general(time, mine, NT, precision=HIGH, preferred_element_type=F32)
    sk_ref[...] = lax.dot_general(sw_ref[...], mine.astype(BF16), NT, preferred_element_type=F32).astype(BF16)


def order_select():
    row = iota((C, 1), 0)
    owner = jnp.zeros((C, 1), jnp.int32)
    for i in range(1, NA):
        owner = jnp.where(row >= CX * i, i, owner)
    row = row - CX * owner
    target = 40 * (row & 15) + 5 * owner + (row >> 4)
    return jnp.where(target == iota((C, C), 1), 1.0, 0.0).astype(BF16)


def conv_body(idx_ref, ker_ref, far_ref, tok_ref, skip_ref, time_ref, gain_ref, shift_ref, send_ref, own_ref, ker_f32):
    b = idx_ref[0]
    core = idx_ref[2]
    for n, ref in enumerate((ker_ref, far_ref)):
        for strip in range(4):
            ker_f32[n, strip] = ref[:, :, 128 * strip : 128 * strip + 128].astype(F32).reshape(NB * TOK, 128)
    stats = jnp.zeros((1, 128), F32)
    for j in range(NA):
        stats = stats + jnp.sum(tok_ref[j, 32:48, 0:128].astype(F32)[8:11], axis=0, keepdims=True)
    wide = spread_sums(stats, in_select((128, C_IN), 0, 1)) / COUNT_IN
    gain = gain_ref[...]
    shift = shift_ref[...]

    def act(values, s):
        mean = wide[2 * s : 2 * s + 1]
        spread = wide[2 * s + 1 : 2 * s + 2] - mean * mean
        n = (values - mean) * lax.rsqrt(spread + EPS) * gain + shift
        n = n / (1.0 + jnp.exp(-n))
        return n.astype(BF16).astype(F32)

    x1 = jnp.concatenate([tok_ref[j, 0:16, :] for j in range(NA)], axis=0)
    x2 = jnp.concatenate([tok_ref[j, 16:32, :] for j in range(NA)], axis=0)
    top = tok_ref[0, 32:48, :].astype(F32)[0:8]
    bottom = tok_ref[NA - 1, 32:48, :].astype(F32)[0:8]
    a1 = act(x1.astype(F32), 0)
    a2 = act(x2.astype(F32), 1)
    top = jnp.where(b == 0, 0.0, act(top, 0))
    bottom = jnp.where(b == NB - 1, 0.0, act(bottom, 0))
    a1 = jnp.concatenate([top, a1, bottom], axis=0)

    def near_first(a):
        swapped = jnp.concatenate([a[:, HALF:], a[:, :HALF]], axis=1)
        return jnp.where(core == 0, a, swapped)

    a1 = near_first(a1)
    a2 = near_first(a2)

    def columns(a):
        n = a.shape[0]
        col = iota(a.shape, 0) & 7
        left = jnp.where(col == 0, 0.0, pltpu.roll(a, 1, 0))
        right = jnp.where(col == 7, 0.0, pltpu.roll(a, n - 1, 0))
        return (left, a, right)

    cols1 = columns(a1)
    cols2 = columns(a2)
    rows = 2 * NA
    acc = jnp.dot(jnp.concatenate([x1, x2], axis=0), skip_ref[...], preferred_element_type=F32)
    conv = jnp.zeros((2 * NA * TOK, CX), F32)
    for dy in range(3):
        for dx in range(3):
            b1, b2 = cols1[dx], cols2[dx]
            first = b1[8 * dy : 8 * dy + 8 * rows]
            tiles = []
            for r in range(rows):
                stale = (dy == 0 and r % 2 == 0) or (dy == 2 and r % 2 == 1)
                at = r + dy - 1
                tiles.append(b1[8 * at + 8 : 8 * at + 16] if stale else b2[8 * at : 8 * at + 8])
            taps = jnp.concatenate([first] + tiles, axis=0).astype(BF16)
            t = 3 * dy + dx
            slab = []
            for k in range(5):
                third, row = divmod(5 * t + k, 15)
                strip, off = divmod(HALF * third, 128)
                ends = []
                for n in range(2):
                    pair = [ker_f32[n, strip + e, pl.ds(row, NB, stride=TOK), :] for e in range(2)]
                    ends.append(jnp.concatenate(pair, axis=1)[:, off : off + HALF])
                slab.append(jnp.concatenate(ends, axis=1))
            slab = jnp.concatenate(slab, axis=0).astype(BF16)
            conv = conv + lax.dot_general(taps, slab, NT, preferred_element_type=F32)
    half = NA * TOK
    step = iota((2 * half, 1), 0) >= half
    h = acc + conv + jnp.where(step, time_ref[1:2, :], time_ref[0:1, :])
    h = h.astype(BF16).astype(F32)
    h1 = h[:half]
    h2 = h[half:]
    sums = [jnp.sum(v, axis=0, keepdims=True) for v in (h1, h1 * h1, h2, h2 * h2)]
    sums = jnp.concatenate(sums + [jnp.zeros((4, CX), F32)], axis=0)
    group = 2 * (iota((CX, GROUPS), 0) & 15) + (idx_ref[1] >> 2)
    select = (group == iota((CX, GROUPS), 1)).astype(F32)
    sums = jnp.dot(sums, select, precision=HIGH, preferred_element_type=F32)
    side = jnp.concatenate([p[0:4] for p in pieces(sums)] + [jnp.zeros((4, GROUPS), F32)], axis=0)
    rest = jnp.zeros((TOK, 128 - CX - GROUPS), F32)
    blocks = [jnp.concatenate([h1[TOK * j : TOK * j + TOK], side, rest], axis=1).astype(BF16) for j in range(NA)]

    def put(i, carry):
        for j in range(NA):
            send_ref[NA * i + j] = blocks[j]
        return carry

    lax.fori_loop(0, NB, put, 0)
    both = [jnp.concatenate([v[TOK * j : TOK * j + TOK] for j in range(NA)], axis=1) for v in (h1, h2)]
    own_ref[...] = jnp.concatenate(both, axis=0).astype(BF16)


def group_body(idx_ref, h_ref, rows_ref, base_ref):
    pair = idx_ref[1] >> 2
    order = order_select()
    blocks = [h_ref[i % 4, pair if i < 4 else 1 - pair] for i in range(NA)]
    rows = []
    for j in range(NA):
        rows.append(jnp.concatenate([block[:, CX * j : CX * j + CX] for block in blocks], axis=1))
    rows = jnp.concatenate(rows, axis=0)
    rows_ref[...] = jnp.dot(rows, order, preferred_element_type=F32).astype(BF16)
    own = pl.multiple_of(2 * TOK * idx_ref[1], 2 * TOK)
    base_ref[...] = rows_ref[pl.ds(own, 2 * TOK), :].astype(F32)


def attend_body(idx_ref, h_ref, rows_ref, qw_ref, kw_ref, vw_ref, gain_ref, shift_ref, send_ref, kk_ref, vv_ref, mq_ref):
    b = idx_ref[0]
    x = idx_ref[1]
    sums = jnp.sum(h_ref[...].astype(F32), axis=0)[:, CX : CX + GROUPS]
    sums = jnp.concatenate([sums[0:4] + sums[4:8] + sums[8:12], jnp.zeros((4, GROUPS), F32)], axis=0)
    group = 20 * iota((GROUPS, C), 0)
    channel = iota((GROUPS, C), 1)
    select = ((channel >= group) & (channel < group + 20)).astype(F32)
    wide = jnp.dot(sums, select, precision=HIGH, preferred_element_type=F32) / COUNT_MID
    mean1, mean2 = wide[0:1], wide[2:3]
    rstd1 = lax.rsqrt(wide[1:2] - mean1 * mean1 + EPS)
    rstd2 = lax.rsqrt(wide[3:4] - mean2 * mean2 + EPS)
    gain = gain_ref[...]
    shift = shift_ref[...]

    def norm(h, mean, rstd):
        return (((h - mean) * rstd) * gain + shift).astype(BF16)

    def project(m, ref):
        return lax.dot_general(m, ref[...], NT, preferred_element_type=F32).astype(BF16)

    keys = []
    for n in range(NB):
        keys.append(jnp.concatenate([h_ref[NA * n + i, :, 0:CX] for i in range(NA)], axis=1))
    keys = jnp.concatenate(keys, axis=0)
    keys = norm(jnp.dot(keys, order_select(), preferred_element_type=F32), mean1, rstd1)
    second = ((iota((NA * 2 * TOK, 1), 0) >> 4) & 1) == 1
    mean = jnp.where(second, mean2, mean1)
    rstd = jnp.where(second, rstd2, rstd1)
    mq_ref[...] = norm(rows_ref[...].astype(F32), mean, rstd)
    queries = project(mq_ref[...], qw_ref)
    fresh = mq_ref[pl.ds(pl.multiple_of(2 * TOK * x + TOK, TOK), TOK), :]
    for ref, weight in ((kk_ref, kw_ref), (vv_ref, vw_ref)):
        ref[0:KEYS_DEV, :] = project(keys, weight)
        ref[KEYS_DEV : KEYS_DEV + TOK, :] = project(fresh, weight)
        ref[KEYS_DEV + TOK :, :] = jnp.zeros((KEYS_PAD - KEYS_DEV - TOK, ATT), BF16)
    each = NA * 2 * TOK
    rows = HEADS * each
    q = queries.astype(F32) * (1.0 / math.sqrt(HEAD))
    lane_head = iota((each, ATT), 1) >> 6
    q = jnp.concatenate([jnp.where(lane_head == n, q, 0.0) for n in range(HEADS)], axis=0).astype(BF16)
    scores = lax.dot_general(q, kk_ref[...], NT, preferred_element_type=F32)
    col = iota((1, KEYS_PAD), 1)
    row = iota((rows, 1), 0)
    later = (((row >> 4) & 1) == 1) & (((row >> 5) & (NA - 1)) == x)
    low = b * TOK
    stale = (col >= low) & (col < low + TOK)
    usual = jnp.where(col < KEYS_DEV, 0.0, -1e30)
    special = jnp.where(stale | (col >= KEYS_DEV + TOK), -1e30, 0.0)
    scores = scores + jnp.where(later, special, usual)
    top = jnp.max(scores, axis=1, keepdims=True)
    weights = jnp.exp(scores - top)
    denom = jnp.sum(weights, axis=1, keepdims=True)
    mixed = jnp.dot(weights.astype(BF16), vv_ref[...], preferred_element_type=F32)
    out = jnp.zeros((each, ATT), F32)
    side = jnp.zeros((each, HEAD), F32)
    place = iota((each, HEAD), 1)
    split = pieces(top) + pieces(denom)
    for n in range(HEADS):
        at = slice(each * n, each * n + each)
        out = jnp.where(lane_head == n, mixed[at], out)
        for p in range(6):
            side = jnp.where(place == 8 * p + n, split[p][at], side)
    out = jnp.concatenate([out, side], axis=1).astype(BF16)
    for j in range(NA):
        send_ref[j] = out[2 * TOK * j : 2 * TOK * j + 2 * TOK]


def combine_body(part_ref, base_ref, ow_ref, o1_ref, o2_ref):
    sides = part_ref[:, :, ATT:].reshape(NA * 2 * TOK, HEAD)
    place = iota((HEAD, ATT), 0)
    same = (place & 7) == (iota((HEAD, ATT), 1) >> 6)
    tops = jnp.dot(sides, (same & (place < 24)).astype(BF16), preferred_element_type=F32)
    denoms = jnp.dot(sides, (same & (place >= 24) & (place < 48)).astype(BF16), preferred_element_type=F32)

    def of(values, i):
        return values[2 * TOK * i : 2 * TOK * i + 2 * TOK]

    top = of(tops, 0)
    for i in range(1, NA):
        top = jnp.maximum(top, of(tops, i))
    mixed = jnp.zeros((2 * TOK, ATT), F32)
    denom = jnp.zeros((2 * TOK, ATT), F32)
    for i in range(NA):
        factor = jnp.exp(of(tops, i) - top)
        mixed = mixed + part_ref[i, :, 0:ATT].astype(F32) * factor
        denom = denom + of(denoms, i) * factor
    out = (mixed / denom).astype(BF16)
    result = base_ref[...] + jnp.dot(out, ow_ref[...], preferred_element_type=F32)
    result = result.astype(BF16)
    o1_ref[...] = result[0:TOK]
    o2_ref[...] = result[TOK:]


def call(body, out_shape, in_specs, scratch=(), cost=None):
    many = isinstance(out_shape, (list, tuple))
    vmem = pl.BlockSpec(memory_space=pltpu.VMEM)
    return pl.pallas_call(
        body,
        out_shape=out_shape,
        in_specs=in_specs,
        out_specs=[vmem] * len(out_shape) if many else vmem,
        scratch_shapes=list(scratch),
        compiler_params=pltpu.CompilerParams(vmem_limit_bytes=VMEM_LIMIT),
        cost_estimate=cost,
    )


def shape(dims, dtype=BF16):
    return jax.ShapeDtypeStruct(dims, dtype)


def spread(blocks, axis):
    return lax.all_to_all(blocks, axis, 0, 0, tiled=True)


def time_features(steps_int, width):
    half = width // 2
    freqs = jnp.exp(-math.log(10000.0) * jnp.arange(half, dtype=F32) / half)
    angles = steps_int.astype(F32)[:, None] * freqs[None, :]
    return jnp.concatenate([jnp.cos(angles), jnp.sin(angles)], axis=1)


def per_device(
    x_first,
    x_second,
    timesteps,
    conv_kernel,
    skip_weight,
    time_weight,
    gain_in,
    shift_in,
    gain_mid,
    shift_mid,
    query_weight,
    key_weight,
    value_weight,
    out_weight,
):
    vmem = pl.BlockSpec(memory_space=pltpu.VMEM)
    smem = pl.BlockSpec(memory_space=pltpu.SMEM)
    b = lax.axis_index("b")
    x = lax.axis_index(A)
    idx = jnp.stack([b, x, lax.axis_index("core")]).astype(jnp.int32)
    x1 = x_first.reshape(TOK, C_IN)
    x2 = x_second.reshape(TOK, C_IN)

    whole = lambda *dims: pl.BlockSpec(dims, lambda i: (0,) * len(dims))
    first, edge = pl.pallas_call(
        pack_kernel_body,
        grid=(1,),
        out_shape=[shape((NB, TOK, 512)), shape((8, C_IN))],
        in_specs=[smem, whole(TOK, C_IN), whole(TOK, C_IN), whole(9, 5, C_IN)],
        out_specs=[whole(NB, TOK, 512), whole(8, C_IN)],
        scratch_shapes=[pltpu.VMEM((BLK, HALF), F32), pltpu.VMEM((TOK, 512), F32)],
        compiler_params=pltpu.CompilerParams(vmem_limit_bytes=3 * VMEM_LIMIT),
    )(idx, x1, x2, jnp.transpose(conv_kernel, (1, 0, 2)))
    pairs = []
    for g in range(NB - 1):
        pairs += [(NA * g + NA - 1, NA * g + NA), (NA * g + NA, NA * g + NA - 1)]
    halo = lax.ppermute(edge, ("b",) + A, pairs)
    kernels = spread(first, "b")

    feats = jax.nn.silu(time_features(timesteps, C_IN))
    feats = jnp.pad(feats, ((0, 6), (0, 0)))
    skip_slab, time_slab = call(
        slabs_body,
        [shape((C_IN, CX)), shape((8, CX), F32)],
        [smem] + [vmem] * 3,
        cost=pl.CostEstimate(flops=2 * 640 * 320 * 200, bytes_accessed=1 << 20, transcendentals=0),
    )(idx, feats, time_weight, skip_weight)

    tokens, again = call(tokens_body, [shape((NA, BLK, C_IN)), shape((NB, TOK, 512))], [vmem] * 5)(
        kernels, x1, x2, halo, time_slab
    )
    far = lax.ppermute(again, "core", [(0, 1), (1, 0)])
    tokens = spread(tokens, A)

    send, own = call(
        conv_body,
        [shape((NB * NA, TOK, 128)), shape((2 * TOK, C))],
        [smem] + [vmem] * 7,
        [pltpu.VMEM((2, 4, NB * TOK, 128), F32)],
    )(idx, kernels, far, tokens, skip_slab, time_slab, gain_in[None], shift_in[None])
    other = lax.ppermute(own, "p", [(0, 1), (1, 0)])
    everyone = spread(send, ("b",) + A)
    group = lax.all_gather(jnp.concatenate([own, other], axis=0), "x", axis=0, tiled=True)
    rows, base = call(
        group_body,
        [shape((NA * 2 * TOK, C)), shape((2 * TOK, C), F32)],
        [smem, vmem],
        cost=pl.CostEstimate(flops=2 * 10**10, bytes_accessed=1 << 20, transcendentals=0),
    )(idx, group.reshape(NA // 2, 2, 2 * TOK, C))
    partial = call(
        attend_body,
        shape((NA, 2 * TOK, ATT + HEAD)),
        [smem] + [vmem] * 7,
        [pltpu.VMEM((KEYS_PAD, ATT), BF16), pltpu.VMEM((KEYS_PAD, ATT), BF16), pltpu.VMEM((NA * 2 * TOK, C), BF16)],
    )(idx, everyone, rows, query_weight.T, key_weight.T, value_weight.T, gain_mid[None], shift_mid[None])
    partial = spread(partial, A)
    out1, out2 = call(combine_body, [shape((TOK, C)), shape((TOK, C))], [vmem] * 3)(partial, base, out_weight)
    dims = x_first.shape[:2] + (C,)
    return out1.reshape(dims), out2.reshape(dims)


def solution(mesh):
    grid = Mesh(mesh.devices.reshape(NB, 2, NA // 2, 2, 2), ("b", "p", "x", "y_hi", "core"))
    tokens = P(("y_hi", "core", "b", "p", "x"), None, None)
    return jax.shard_map(
        per_device,
        mesh=grid,
        in_specs=(tokens, tokens, P(), P(("b", "p", "x"), None, None)) + (P(),) * 10,
        out_specs=(tokens, tokens),
        check_vma=False,
    )
```

```python
import functools
import math

import jax
import jax.numpy as jnp
from jax import lax
from jax.experimental import pallas as pl
from jax.experimental.pallas import tpu as pltpu
from jax.sharding import Mesh, PartitionSpec as P

F32 = jnp.float32
BF16 = jnp.bfloat16
HEADS = 5
HEAD = 64
GROUPS = 32
C_IN = 320
C = 640
ATT = HEADS * HEAD
EPS = 1e-05
NB = 16
NA = 8
TOK = 16
CX = C // NA
KEYS = NB * NA * TOK
COUNT_IN = float(KEYS * (C_IN // GROUPS))
COUNT_MID = float(KEYS * (C // GROUPS))
BLK = 48
HALF = C_IN // 2
KEYS_DEV = NB * TOK
KEYS_PAD = KEYS_DEV + 128
COUNT_IN = float(KEYS * (C_IN // GROUPS))
COUNT_MID = float(KEYS * (C // GROUPS))
BLK = 48
HALF = C_IN // 2
KEYS_DEV = NB * TOK
KEYS_PAD = KEYS_DEV + 128
COUNT_IN = float(KEYS * (C_IN // GROUPS))
COUNT_MID = float(KEYS * (C // GROUPS))
BLK = 48
HALF = C_IN // 2
KEYS_DEV = NB * TOK
KEYS_PAD = KEYS_DEV + 128
COUNT_IN = float(KEYS * (C_IN // GROUPS))
COUNT_MID = float(KEYS * (C // GROUPS))
BLK = 48
HALF = C_IN // 2
KEYS_DEV = NB * TOK
KEYS_PAD = KEYS_DEV + 128
PACK = KEYS_DEV // NA
RELAY = PACK + 3 * TOK
A = ("p", "x")
HIGH = lax.Precision.HIGHEST
NT = (((1,), (1,)), ((), ()))
VMEM_LIMIT = 20 * 1024 * 1024


def iota(shape, dim):
    return lax.broadcasted_iota(jnp.int32, shape, dim)


def pieces(row):
    hi = row.astype(BF16).astype(F32)
    mid = (row - hi).astype(BF16).astype(F32)
    lo = (row - hi - mid).astype(BF16).astype(F32)
    return hi, mid, lo


def fold_sums(rows, select):
    wide = jnp.dot(rows, select, precision=HIGH, preferred_element_type=F32)
    keep = (iota((8, 128), 1) >> 5) == iota((8, 128), 0)
    return jnp.sum(jnp.where(keep, wide, 0.0), axis=0, keepdims=True)


def spread_sums(line, select):
    keep = (iota((8, 128), 1) >> 5) == iota((8, 128), 0)
    rows = jnp.where(keep, jnp.broadcast_to(line, (8, 128)), 0.0)
    return jnp.dot(rows, select, precision=HIGH, preferred_element_type=F32)


def in_select(shape, group_dim, channel_dim):
    group = iota(shape, group_dim) & 31
    channel = iota(shape, channel_dim)
    return ((channel >= 10 * group) & (channel < 10 * group + 10)).astype(F32)


def slab_select(shape, x, dtype):
    row = iota(shape, 0)
    target = 40 * (row & 15) + 5 * x + (row >> 4)
    return (target == iota(shape, 1)).astype(dtype)


def pack_kernel_body(idx_ref, x1_ref, x2_ref, ker_ref, out_ref, edge_ref, rows_ref, lanes_ref):
    core = idx_ref[2]
    for t in range(9):
        both = ker_ref[t].astype(F32)
        rows_ref[5 * t : 5 * t + 5, :] = jnp.where(core == 0, both[:, :HALF], both[:, HALF:])
    x1 = x1_ref[...].astype(F32)
    x2 = x2_ref[...].astype(F32)
    edge_ref[...] = jnp.where(idx_ref[1] == NA - 1, x1[8:16], x1[0:8]).astype(BF16)
    sums = [jnp.sum(v, axis=0, keepdims=True) for v in (x1, x1 * x1, x2, x2 * x2)]
    sums = jnp.concatenate(sums + [jnp.zeros((4, C_IN), F32)], axis=0)
    line = fold_sums(sums, in_select((C_IN, 128), 1, 0))
    thirds = [rows_ref[15 * b : 15 * b + 15, :] for b in range(3)]
    lanes_ref[0:15, :] = jnp.concatenate(thirds + [jnp.zeros((15, 32), F32)], axis=1)
    lanes_ref[15:16, :] = jnp.concatenate(list(pieces(line)) + [jnp.zeros((1, 128), F32)], axis=1)
    block = lanes_ref[...].astype(BF16)

    def put(i, carry):
        out_ref[i] = block
        return carry

    lax.fori_loop(0, NB, put, 0)


def tokens_body(part_ref, x1_ref, x2_ref, halo_ref, after_ref, out_ref):
    part = jnp.sum(part_ref[:, :, 0:384].astype(F32), axis=0)[15:16]
    hi, mid, lo = pieces(part[:, 0:128] + part[:, 128:256] + part[:, 256:384])
    stats = jnp.concatenate([hi, mid, lo, jnp.zeros((5, 128), F32)], axis=0)
    stats = jnp.concatenate([stats, jnp.zeros((8, C_IN - 128), F32)], axis=1)
    tail = jnp.concatenate([halo_ref[...].astype(F32), stats], axis=0).astype(BF16)
    for i in range(NA):
        out_ref[i, 0:16, :] = x1_ref[...]
        out_ref[i, 16:32, :] = x2_ref[...]
        out_ref[i, 32:48, :] = tail


def slabs_body(idx_ref, feats_ref, tw_ref, sw_ref, sk_ref, tm_ref, order_ref):
    order_ref[...] = order_select()
    mine = slab_select((CX, C), idx_ref[1], F32)
    time = jnp.dot(feats_ref[...], tw_ref[...].astype(F32), precision=HIGH, preferred_element_type=F32)
    tm_ref[...] = lax.dot_general(time, mine, NT, precision=HIGH, preferred_element_type=F32)
    sk_ref[...] = lax.dot_general(sw_ref[...], mine.astype(BF16), NT, preferred_element_type=F32).astype(BF16)


def order_select():
    row = iota((C, 1), 0)
    owner = jnp.zeros((C, 1), jnp.int32)
    for i in range(1, NA):
        owner = jnp.where(row >= CX * i, i, owner)
    row = row - CX * owner
    target = 40 * (row & 15) + 5 * owner + (row >> 4)
    return jnp.where(target == iota((C, C), 1), 1.0, 0.0).astype(BF16)


def conv_body(idx_ref, ker_ref, far_ref, tok_ref, skip_ref, time_ref, gain_ref, shift_ref, send_ref, own_ref, ker_f32):
    b = idx_ref[0]
    core = idx_ref[2]
    for n, ref in enumerate((ker_ref, far_ref)):
        for strip in range(4):
            ker_f32[n, strip] = ref[:, :, 128 * strip : 128 * strip + 128].astype(F32).reshape(NB * TOK, 128)
    stats = jnp.zeros((1, 128), F32)
    for j in range(NA):
        stats = stats + jnp.sum(tok_ref[j, 32:48, 0:128].astype(F32)[8:11], axis=0, keepdims=True)
    wide = spread_sums(stats, in_select((128, C_IN), 0, 1)) / COUNT_IN
    gain = gain_ref[...]
    shift = shift_ref[...]

    def act(values, s):
        mean = wide[2 * s : 2 * s + 1]
        spread = wide[2 * s + 1 : 2 * s + 2] - mean * mean
        n = (values - mean) * lax.rsqrt(spread + EPS) * gain + shift
        n = n / (1.0 + jnp.exp(-n))
        return n.astype(BF16).astype(F32)

    x1 = jnp.concatenate([tok_ref[j, 0:16, :] for j in range(NA)], axis=0)
    x2 = jnp.concatenate([tok_ref[j, 16:32, :] for j in range(NA)], axis=0)
    top = tok_ref[0, 32:48, :].astype(F32)[0:8]
    bottom = tok_ref[NA - 1, 32:48, :].astype(F32)[0:8]
    a1 = act(x1.astype(F32), 0)
    a2 = act(x2.astype(F32), 1)
    top = jnp.where(b == 0, 0.0, act(top, 0))
    bottom = jnp.where(b == NB - 1, 0.0, act(bottom, 0))
    a1 = jnp.concatenate([top, a1, bottom], axis=0)

    def near_first(a):
        swapped = jnp.concatenate([a[:, HALF:], a[:, :HALF]], axis=1)
        return jnp.where(core == 0, a, swapped)

    a1 = near_first(a1)
    a2 = near_first(a2)

    def columns(a):
        n = a.shape[0]
        col = iota(a.shape, 0) & 7
        left = jnp.where(col == 0, 0.0, pltpu.roll(a, 1, 0))
        right = jnp.where(col == 7, 0.0, pltpu.roll(a, n - 1, 0))
        return (left, a, right)

    cols1 = columns(a1)
    cols2 = columns(a2)
    rows = 2 * NA
    acc = jnp.dot(jnp.concatenate([x1, x2], axis=0), skip_ref[...], preferred_element_type=F32)
    conv = jnp.zeros((2 * NA * TOK, CX), F32)
    for dy in range(3):
        for dx in range(3):
            b1, b2 = cols1[dx], cols2[dx]
            first = b1[8 * dy : 8 * dy + 8 * rows]
            tiles = []
            for r in range(rows):
                stale = (dy == 0 and r % 2 == 0) or (dy == 2 and r % 2 == 1)
                at = r + dy - 1
                tiles.append(b1[8 * at + 8 : 8 * at + 16] if stale else b2[8 * at : 8 * at + 8])
            taps = jnp.concatenate([first] + tiles, axis=0).astype(BF16)
            t = 3 * dy + dx
            slab = []
            for k in range(5):
                third, row = divmod(5 * t + k, 15)
                strip, off = divmod(HALF * third, 128)
                ends = []
                for n in range(2):
                    pair = [ker_f32[n, strip + e, pl.ds(row, NB, stride=TOK), :] for e in range(2)]
                    ends.append(jnp.concatenate(pair, axis=1)[:, off : off + HALF])
                slab.append(jnp.concatenate(ends, axis=1))
            slab = jnp.concatenate(slab, axis=0).astype(BF16)
            conv = conv + lax.dot_general(taps, slab, NT, preferred_element_type=F32)
    half = NA * TOK
    step = iota((2 * half, 1), 0) >= half
    h = acc + conv + jnp.where(step, time_ref[1:2, :], time_ref[0:1, :])
    h = h.astype(BF16).astype(F32)
    h1 = h[:half]
    h2 = h[half:]
    sums = [jnp.sum(v, axis=0, keepdims=True) for v in (h1, h1 * h1, h2, h2 * h2)]
    sums = jnp.concatenate(sums + [jnp.zeros((4, CX), F32)], axis=0)
    group = 2 * (iota((CX, GROUPS), 0) & 15) + (idx_ref[1] >> 2)
    select = (group == iota((CX, GROUPS), 1)).astype(F32)
    sums = jnp.dot(sums, select, precision=HIGH, preferred_element_type=F32)
    side = jnp.concatenate([p[0:4] for p in pieces(sums)] + [jnp.zeros((4, GROUPS), F32)], axis=0)
    rest = jnp.zeros((TOK, 128 - CX - GROUPS), F32)
    blocks = [jnp.concatenate([h1[TOK * j : TOK * j + TOK], side, rest], axis=1).astype(BF16) for j in range(NA)]

    def put(i, carry):
        for j in range(NA):
            send_ref[NA * i + j] = blocks[j]
        return carry

    lax.fori_loop(0, NB, put, 0)
    both = [jnp.concatenate([v[TOK * j : TOK * j + TOK] for j in range(NA)], axis=1) for v in (h1, h2)]
    own_ref[...] = jnp.concatenate(both, axis=0).astype(BF16)


def group_body(idx_ref, h_ref, order_ref, rows_ref, base_ref):
    pair = idx_ref[1] >> 2
    blocks = [h_ref[i % 4, pair if i < 4 else 1 - pair] for i in range(NA)]
    rows = []
    for j in range(NA):
        rows.append(jnp.concatenate([block[:, CX * j : CX * j + CX] for block in blocks], axis=1))
    rows = jnp.concatenate(rows, axis=0)
    rows_ref[...] = jnp.dot(rows, order_ref[...], preferred_element_type=F32).astype(BF16)
    own = pl.multiple_of(2 * TOK * idx_ref[1], 2 * TOK)
    base_ref[...] = rows_ref[pl.ds(own, 2 * TOK), :].astype(F32)


def attend_body(idx_ref, h_ref, rows_ref, order_ref, qw_ref, kw_ref, vw_ref, gain_ref, shift_ref, send_ref, kk_ref, vv_ref, mq_ref):
    b = idx_ref[0]
    x = idx_ref[1]
    sums = jnp.sum(h_ref[...].astype(F32), axis=0)[:, CX : CX + GROUPS]
    sums = jnp.concatenate([sums[0:4] + sums[4:8] + sums[8:12], jnp.zeros((4, GROUPS), F32)], axis=0)
    group = 20 * iota((GROUPS, C), 0)
    channel = iota((GROUPS, C), 1)
    select = ((channel >= group) & (channel < group + 20)).astype(F32)
    wide = jnp.dot(sums, select, precision=HIGH, preferred_element_type=F32) / COUNT_MID
    mean1, mean2 = wide[0:1], wide[2:3]
    rstd1 = lax.rsqrt(wide[1:2] - mean1 * mean1 + EPS)
    rstd2 = lax.rsqrt(wide[3:4] - mean2 * mean2 + EPS)
    gain = gain_ref[...]
    shift = shift_ref[...]

    def norm(h, mean, rstd):
        return (((h - mean) * rstd) * gain + shift).astype(BF16)

    def project(m, ref):
        return lax.dot_general(m, ref[...], NT, preferred_element_type=F32).astype(BF16)

    keys = []
    for n in range(NB):
        keys.append(jnp.concatenate([h_ref[NA * n + i, :, 0:CX] for i in range(NA)], axis=1))
    keys = jnp.concatenate(keys, axis=0)
    keys = norm(jnp.dot(keys, order_ref[...], preferred_element_type=F32), mean1, rstd1)
    second = ((iota((NA * 2 * TOK, 1), 0) >> 4) & 1) == 1
    mean = jnp.where(second, mean2, mean1)
    rstd = jnp.where(second, rstd2, rstd1)
    mq_ref[...] = norm(rows_ref[...].astype(F32), mean, rstd)
    queries = project(mq_ref[...], qw_ref)
    fresh = mq_ref[pl.ds(pl.multiple_of(2 * TOK * x + TOK, TOK), TOK), :]
    for ref, weight in ((kk_ref, kw_ref), (vv_ref, vw_ref)):
        ref[0:KEYS_DEV, :] = project(keys, weight)
        ref[KEYS_DEV : KEYS_DEV + TOK, :] = project(fresh, weight)
        ref[KEYS_DEV + TOK :, :] = jnp.zeros((KEYS_PAD - KEYS_DEV - TOK, ATT), BF16)
    each = NA * 2 * TOK
    rows = HEADS * each
    q = queries.astype(F32) * (1.0 / math.sqrt(HEAD))
    lane_head = iota((each, ATT), 1) >> 6
    q = jnp.concatenate([jnp.where(lane_head == n, q, 0.0) for n in range(HEADS)], axis=0).astype(BF16)
    scores = lax.dot_general(q, kk_ref[...], NT, preferred_element_type=F32)
    col = iota((1, KEYS_PAD), 1)
    row = iota((rows, 1), 0)
    later = (((row >> 4) & 1) == 1) & (((row >> 5) & (NA - 1)) == x)
    low = b * TOK
    stale = (col >= low) & (col < low + TOK)
    usual = jnp.where(col < KEYS_DEV, 0.0, -1e30)
    special = jnp.where(stale | (col >= KEYS_DEV + TOK), -1e30, 0.0)
    scores = scores + jnp.where(later, special, usual)
    top = jnp.max(scores, axis=1, keepdims=True)
    weights = jnp.exp(scores - top)
    denom = jnp.sum(weights, axis=1, keepdims=True)
    mixed = jnp.dot(weights.astype(BF16), vv_ref[...], preferred_element_type=F32)
    out = jnp.zeros((each, ATT), F32)
    side = jnp.zeros((each, HEAD), F32)
    place = iota((each, HEAD), 1)
    for n in range(HEADS):
        at = slice(each * n, each * n + each)
        out = jnp.where(lane_head == n, mixed[at], out)
        side = jnp.where((place & 7) == n, jnp.where(place < 24, top[at], denom[at]), side)
    hi, mid, lo = pieces(side)
    third = place >> 3
    side = jnp.where((third == 1) | (third == 4), mid, jnp.where((third == 2) | (third == 5), lo, hi))
    out = jnp.concatenate([out, side], axis=1).astype(BF16)
    for j in range(NA):
        send_ref[j] = out[2 * TOK * j : 2 * TOK * j + 2 * TOK]


def combine_body(part_ref, base_ref, ow_ref, o1_ref, o2_ref):
    sides = part_ref[:, :, ATT:].reshape(NA * 2 * TOK, HEAD)
    place = iota((HEAD, ATT), 0)
    same = (place & 7) == (iota((HEAD, ATT), 1) >> 6)
    tops = jnp.dot(sides, (same & (place < 24)).astype(BF16), preferred_element_type=F32)
    denoms = jnp.dot(sides, (same & (place >= 24) & (place < 48)).astype(BF16), preferred_element_type=F32)

    def of(values, i):
        return values[2 * TOK * i : 2 * TOK * i + 2 * TOK]

    top = of(tops, 0)
    for i in range(1, NA):
        top = jnp.maximum(top, of(tops, i))
    mixed = jnp.zeros((2 * TOK, ATT), F32)
    denom = jnp.zeros((2 * TOK, ATT), F32)
    for i in range(NA):
        factor = jnp.exp(of(tops, i) - top)
        mixed = mixed + part_ref[i, :, 0:ATT].astype(F32) * factor
        denom = denom + of(denoms, i) * factor
    out = (mixed / denom).astype(BF16)
    result = base_ref[...] + jnp.dot(out, ow_ref[...], preferred_element_type=F32)
    result = result.astype(BF16)
    o1_ref[...] = result[0:TOK]
    o2_ref[...] = result[TOK:]


def call(body, out_shape, in_specs, scratch=(), cost=None):
    many = isinstance(out_shape, (list, tuple))
    vmem = pl.BlockSpec(memory_space=pltpu.VMEM)
    return pl.pallas_call(
        body,
        out_shape=out_shape,
        in_specs=in_specs,
        out_specs=[vmem] * len(out_shape) if many else vmem,
        scratch_shapes=list(scratch),
        compiler_params=pltpu.CompilerParams(vmem_limit_bytes=VMEM_LIMIT),
        cost_estimate=cost,
    )


def shape(dims, dtype=BF16):
    return jax.ShapeDtypeStruct(dims, dtype)


def spread(blocks, axis):
    return lax.all_to_all(blocks, axis, 0, 0, tiled=True)


def time_features(steps_int, width):
    half = width // 2
    freqs = jnp.exp(-math.log(10000.0) * jnp.arange(half, dtype=F32) / half)
    angles = steps_int.astype(F32)[:, None] * freqs[None, :]
    return jnp.concatenate([jnp.cos(angles), jnp.sin(angles)], axis=1)


def per_device(
    x_first,
    x_second,
    timesteps,
    conv_kernel,
    skip_weight,
    time_weight,
    gain_in,
    shift_in,
    gain_mid,
    shift_mid,
    query_weight,
    key_weight,
    value_weight,
    out_weight,
):
    vmem = pl.BlockSpec(memory_space=pltpu.VMEM)
    smem = pl.BlockSpec(memory_space=pltpu.SMEM)
    b = lax.axis_index("b")
    x = lax.axis_index(A)
    idx = jnp.stack([b, x, lax.axis_index("core")]).astype(jnp.int32)
    x1 = x_first.reshape(TOK, C_IN)
    x2 = x_second.reshape(TOK, C_IN)

    whole = lambda *dims: pl.BlockSpec(dims, lambda i: (0,) * len(dims))
    first, edge = pl.pallas_call(
        pack_kernel_body,
        grid=(1,),
        out_shape=[shape((NB, TOK, 512)), shape((8, C_IN))],
        in_specs=[smem, whole(TOK, C_IN), whole(TOK, C_IN), whole(9, 5, C_IN)],
        out_specs=[whole(NB, TOK, 512), whole(8, C_IN)],
        scratch_shapes=[pltpu.VMEM((BLK, HALF), F32), pltpu.VMEM((TOK, 512), F32)],
        compiler_params=pltpu.CompilerParams(vmem_limit_bytes=3 * VMEM_LIMIT),
    )(idx, x1, x2, jnp.transpose(conv_kernel, (1, 0, 2)))
    pairs = []
    for g in range(NB - 1):
        pairs += [(NA * g + NA - 1, NA * g + NA), (NA * g + NA, NA * g + NA - 1)]
    halo = lax.ppermute(edge, ("b",) + A, pairs)
    kernels = spread(first, "b")

    feats = jax.nn.silu(time_features(timesteps, C_IN))
    feats = jnp.pad(feats, ((0, 6), (0, 0)))
    skip_slab, time_slab, order = call(
        slabs_body,
        [shape((C_IN, CX)), shape((8, CX), F32), shape((C, C))],
        [smem] + [vmem] * 3,
        cost=pl.CostEstimate(flops=2 * 640 * 320 * 200, bytes_accessed=1 << 20, transcendentals=0),
    )(idx, feats, time_weight, skip_weight)

    tokens = call(tokens_body, shape((NA, BLK, C_IN)), [vmem] * 5)(
        kernels, x1, x2, halo, time_slab
    )
    far = lax.ppermute(kernels, "core", [(0, 1), (1, 0)])
    tokens = spread(tokens, A)

    send, own = call(
        conv_body,
        [shape((NB * NA, TOK, 128)), shape((2 * TOK, C))],
        [smem] + [vmem] * 7,
        [pltpu.VMEM((2, 4, NB * TOK, 128), F32)],
    )(idx, kernels, far, tokens, skip_slab, time_slab, gain_in[None], shift_in[None])
    other = lax.ppermute(own, "p", [(0, 1), (1, 0)])
    everyone = spread(send, ("b",) + A)
    group = lax.all_gather(jnp.concatenate([own, other], axis=0), "x", axis=0, tiled=True)
    rows, base = call(
        group_body,
        [shape((NA * 2 * TOK, C)), shape((2 * TOK, C), F32)],
        [smem, vmem, vmem],
        cost=pl.CostEstimate(flops=2 * 10**10, bytes_accessed=1 << 20, transcendentals=0),
    )(idx, group.reshape(NA // 2, 2, 2 * TOK, C), order)
    partial = call(
        attend_body,
        shape((NA, 2 * TOK, ATT + HEAD)),
        [smem] + [vmem] * 8,
        [pltpu.VMEM((KEYS_PAD, ATT), BF16), pltpu.VMEM((KEYS_PAD, ATT), BF16), pltpu.VMEM((NA * 2 * TOK, C), BF16)],
    )(idx, everyone, rows, order, query_weight.T, key_weight.T, value_weight.T, gain_mid[None], shift_mid[None])
    partial = spread(partial, A)
    out1, out2 = call(combine_body, [shape((TOK, C)), shape((TOK, C))], [vmem] * 3)(partial, base, out_weight)
    dims = x_first.shape[:2] + (C,)
    return out1.reshape(dims), out2.reshape(dims)


def solution(mesh):
    grid = Mesh(mesh.devices.reshape(NB, 2, NA // 2, 2, 2), ("b", "p", "x", "y_hi", "core"))
    tokens = P(("y_hi", "core", "b", "p", "x"), None, None)
    return jax.shard_map(
        per_device,
        mesh=grid,
        in_specs=(tokens, tokens, P(), P(("b", "p", "x"), None, None)) + (P(),) * 10,
        out_specs=(tokens, tokens),
        check_vma=False,
    )
```
